32 devices in a mesh: parts: 1, head: 32 (over z, y, x, core).
Axes of the slice: x: 2, y: 2, z: 4, core: 2. Of those that a mesh axis runs over, the one named last changes fastest.
Arguments:
- queries: bfloat16 [8, 2048, 2048], P('parts', 'head'), may hold values from -6 to 6
- keys: bfloat16 [8, 2048, 2048], P('parts', 'head'), may hold values from -6 to 6
- values: bfloat16 [8, 2048, 2048], P('parts', 'head'), may hold values from -6 to 6
- slot_positions: int32 [8, 2048], P('parts', 'head'), may hold values from 0 to 2047, each once within a row
- counts: int32 [8], P('parts'), may hold values from 16 to 2048, as said below
- timesteps: int32 [8], P('parts'), may hold values from 0 to 999
- labels: int32 [8], P('parts'), may hold values from 0 to 127
- time_weight: bfloat16 [256, 4096], replicated, may hold values from -0.375 to 0.375
- norm_gain: float32 [2048], replicated, may hold values from 0.25 to 1.75
- gate_weight: bfloat16 [2048, 8192], P(None, 'head'), may hold values from -0.125 to 0.125
- up_weight: bfloat16 [2048, 8192], P(None, 'head'), may hold values from -0.125 to 0.125
- down_weight: bfloat16 [8192, 2048], P('head'), may hold values from -0.0625 to 0.0625
- class_weight: bfloat16 [2048, 128], replicated, may hold values from -3 to 3
- class_bias: float32 [128], replicated, may hold values from -5 to 112
Outputs:
- attention: bfloat16 [256, 2048, 64], P(('parts', 'head'))
- guidance: float32 [8, 128, 2048], P('parts', 'head')
The draws below stay inside these ranges and needn't reach their ends.
Inputs may be any that keep to these rules, and one draw needn't show every extreme that they name: `counts`: multiples of 16; in every part one shower has exactly 2048. `slot_positions`: each shower's row is a permutation of 0 to 2047.
All inputs are finite; a program needn't handle non-finite values.
Results may differ from the reference program's by a relative error of at most 0.01.
The reference program's roundings to bfloat16 on the way count: a program that leaves them out, or rounds other values in their place, can miss the bound.
Values may be sent and summed in bfloat16 or wider, within the bound.
No kernel may reach another device: no remote copies, remote signals or barrier semaphores. Data moves between devices by JAX's collectives and lax.ppermute only.
A program may use at most 192 MiB of HBM per device.

```python
import math
import jax
import jax.numpy as jnp
from jax import lax

HEADS = 32
HD = 64
CD = 2048
FF = 8192
L = 2048
SH = 8
POOL = 16
FREQ = 256
NT = 1000
CLASSES = 128
PAIRS = 256
WP = 128
ROWS = 1024


def drawn_fields(key):
    field_shape = (SH, L, HEADS * HD)
    query_base = jnp.clip(jax.random.normal(jax.random.fold_in(key, 11), field_shape, jnp.float32), -6.0, 6.0)
    key_base = jnp.clip(jax.random.normal(jax.random.fold_in(key, 12), field_shape, jnp.float32), -6.0, 6.0)
    return (query_base, key_base)


def draw_queries(key, part):
    return drawn_fields(key)[0].astype(jnp.bfloat16)


def draw_keys(key, part):
    return drawn_fields(key)[1].astype(jnp.bfloat16)


def draw_counts(key, part):
    units = jax.random.randint(jax.random.fold_in(key, 21), (SH,), 1, L // POOL + 1)
    fullest = jax.random.randint(jax.random.fold_in(key, 22), (), 0, SH)
    units = jnp.where(jnp.arange(SH) == fullest, L // POOL, units)
    return (units * POOL).astype(jnp.int32)


def draw_class_bias(key, part):
    biases = jnp.clip(jax.random.normal(jax.random.fold_in(key, 31), (CLASSES,), jnp.float32), -5.0, 5.0)
    return biases


def touch_ends(result, key, least, top_value):
    extent = result.shape
    index_at = [jax.random.randint(jax.random.fold_in(key, axis), (), 0, extent[axis]) for axis in range(len(extent))]
    result = result.at[tuple(index_at)].set(least)
    longest = extent.index(max(extent))
    index_at[longest] = (index_at[longest] + 1) % extent[longest]
    return result.at[tuple(index_at)].set(top_value)


def level_of(own_key, extent, cuts, smallest, top_value):
    def one(position, parts):
        draws = jax.random.uniform(jax.random.fold_in(jax.random.fold_in(own_key, 6), position), (parts,), jnp.float32, smallest / len(cuts), top_value / len(cuts))
        return jnp.repeat(jnp.exp(draws), extent[position] // parts).reshape((-1,) + (1,) * (len(extent) - position - 1))

    level = one(*cuts[0])
    for cut in cuts[1:]:
        level = level * one(*cut)
    return level


def scatter_about(key, dims, deviation, limit, pieces=(), kind=jnp.bfloat16):
    values = deviation * jax.random.normal(key, dims, jnp.float32)
    if pieces:
        values = values * level_of(key, dims, pieces, -0.22, 0.18)
    return jnp.clip(values, -limit, limit).astype(kind)


def setup_inputs(seed: int = 0, part: int = 0) -> dict:
    seeds = jax.random.split(jax.random.key(seed), 15)
    part_splits = jax.random.split(jax.random.fold_in(seeds[14], part), 15)
    queries = draw_queries(jax.random.fold_in(jax.random.fold_in(seeds[14], part), 71), part)
    keys = draw_keys(jax.random.fold_in(jax.random.fold_in(seeds[14], part), 71), part)
    values = scatter_about(part_splits[2], (SH, L, CD), 1.0, 6.0, ((1, 32),))
    slot_positions = jax.vmap(lambda own: jax.random.permutation(own, L))(jax.random.split(part_splits[3], SH)).reshape((SH, L)).astype(jnp.int32)
    counts = draw_counts(jax.random.fold_in(jax.random.fold_in(seeds[14], part), 71), part)
    timesteps = touch_ends(jax.random.randint(part_splits[5], (SH,), 0, NT), jax.random.fold_in(part_splits[5], 1), 0, NT - 1).astype(jnp.int32)
    labels = touch_ends(jax.random.randint(part_splits[6], (SH,), 0, CLASSES), jax.random.fold_in(part_splits[6], 1), 0, CLASSES - 1).astype(jnp.int32)
    time_weight = scatter_about(seeds[7], (FREQ, 2 * CD), FREQ ** -0.5, 0.375)
    norm_gain = jnp.clip(1.0 + 0.15 * jax.random.normal(seeds[8], (CD,), jnp.float32), 0.25, 1.75)
    gate_weight = scatter_about(seeds[9], (CD, FF), CD ** -0.5, 0.125, ((1, 32),))
    up_weight = scatter_about(seeds[10], (CD, FF), CD ** -0.5, 0.125, ((1, 32),))
    down_weight = scatter_about(seeds[11], (FF, CD), FF ** -0.5, 0.0625, ((0, 32),))
    class_weight = scatter_about(seeds[12], (CD, CLASSES), 0.5, 3.0)
    class_bias = draw_class_bias(jax.random.fold_in(seeds[14], 71), part)
    return {"queries": queries, "keys": keys, "values": values, "slot_positions": slot_positions, "counts": counts, "timesteps": timesteps, "labels": labels, "time_weight": time_weight, "norm_gain": norm_gain, "gate_weight": gate_weight, "up_weight": up_weight, "down_weight": down_weight, "class_weight": class_weight, "class_bias": class_bias}


epsilon = 1e-06

def sinusoid(steps):
    half_width = FREQ // 2
    frequency = jnp.exp(-math.log(10000.0) * jnp.arange(half_width, dtype=jnp.float32) / half_width)
    angles = steps.astype(jnp.float32)[:, None] * frequency[None, :]
    return jnp.concatenate([jnp.cos(angles), jnp.sin(angles)], axis=1)

def to_pairs(block):
    return block.reshape(SH, L, HEADS, HD).transpose(0, 2, 1, 3).reshape(PAIRS, L, HD)

def attend_pair(pair_data):
    query_rows, key_rows, value_rows, key_valid = pair_data
    scores = jnp.dot(query_rows, key_rows.T, preferred_element_type=jnp.float32) * HD ** (-0.5)
    scores = jnp.where(key_valid[None, :], scores, -jnp.inf)
    peak = lax.optimization_barrier(jnp.max(scores, axis=1, keepdims=True))
    exponent = jnp.exp(scores - peak)
    weights = (exponent / lax.optimization_barrier(jnp.sum(exponent, axis=1, keepdims=True))).astype(jnp.bfloat16)
    mixed = jnp.dot(weights, value_rows, preferred_element_type=jnp.float32)
    return (mixed * key_valid[:, None].astype(jnp.float32)).astype(jnp.bfloat16)

def reference(queries, keys, values, slot_positions, counts, timesteps, labels, time_weight, norm_gain, gate_weight, up_weight, down_weight, class_weight, class_bias):
    valid_slots = slot_positions < counts[:, None]
    pair_valid = jnp.repeat(valid_slots, HEADS, axis=0)
    attention = lax.map(attend_pair, (to_pairs(queries), to_pairs(keys), to_pairs(values), pair_valid))
    slot_flags = pair_valid.astype(jnp.float32)
    window_count = lax.optimization_barrier(jnp.sum(slot_flags.reshape(PAIRS, WP, POOL), axis=2))
    window_sum = lax.optimization_barrier(jnp.sum(attention.astype(jnp.float32).reshape(PAIRS, WP, POOL, HD), axis=2))
    pooled = (window_sum / jnp.maximum(window_count, 1.0)[:, :, None]).astype(jnp.bfloat16)
    pooled_rows = pooled.reshape(SH, HEADS, WP, HD).transpose(0, 2, 1, 3).reshape(SH, WP, CD).astype(jnp.float32)
    row_count = window_count.reshape(SH, HEADS, WP)[:, 0, :]
    embedding = sinusoid(timesteps).astype(jnp.bfloat16)
    modulation = jnp.dot(embedding, time_weight, preferred_element_type=jnp.float32)
    shifts = modulation[:, None, :CD]
    scales = 1.0 + modulation[:, None, CD:]
    inverse_rms = lax.rsqrt(lax.optimization_barrier(jnp.mean(pooled_rows * pooled_rows, axis=2, keepdims=True)) + epsilon)
    unit_rows = pooled_rows * inverse_rms
    normed = (unit_rows * norm_gain * scales + shifts).astype(jnp.bfloat16).reshape(ROWS, CD)
    gate_out = jnp.dot(normed, gate_weight, preferred_element_type=jnp.float32)
    up_out = jnp.dot(normed, up_weight, preferred_element_type=jnp.float32)
    activated = jax.nn.silu(gate_out)
    hidden = (activated * up_out).astype(jnp.bfloat16)
    mlp_out = jnp.dot(hidden, down_weight, preferred_element_type=jnp.float32).reshape(SH, WP, CD)
    shower_counts = counts.astype(jnp.float32)
    features = lax.optimization_barrier(jnp.sum(row_count[:, :, None] * (pooled_rows + mlp_out), axis=1)) / shower_counts[:, None]
    class_matrix = class_weight.astype(jnp.float32)
    logits = jnp.dot(features, class_matrix, precision=lax.Precision.HIGHEST) + class_bias
    exponent = jnp.exp(logits - lax.optimization_barrier(jnp.max(logits, axis=1, keepdims=True)))
    probability = exponent / lax.optimization_barrier(jnp.sum(exponent, axis=1, keepdims=True))
    target = (labels[:, None] == jnp.arange(CLASSES, dtype=jnp.int32)[None, :]).astype(jnp.float32)
    feature_grad = jnp.dot(target - probability, class_matrix.T, precision=lax.Precision.HIGHEST)
    row_grads = row_count[:, :, None] / shower_counts[:, None, None] * feature_grad[:, None, :]
    hidden_grad = jnp.dot(row_grads.astype(jnp.bfloat16).reshape(ROWS, CD), down_weight.T, preferred_element_type=jnp.float32)
    sigmoid_gate = jax.nn.sigmoid(gate_out)
    gate_grad = (hidden_grad * up_out * sigmoid_gate * (1.0 + gate_out * (1.0 - sigmoid_gate))).astype(jnp.bfloat16)
    up_grad = (hidden_grad * activated).astype(jnp.bfloat16)
    normed_grad = jnp.dot(gate_grad, gate_weight.T, preferred_element_type=jnp.float32) + jnp.dot(up_grad, up_weight.T, preferred_element_type=jnp.float32)
    unit_grad = normed_grad.reshape(SH, WP, CD) * norm_gain * scales
    pooled_grad = inverse_rms * (unit_grad - unit_rows * lax.optimization_barrier(jnp.mean(unit_grad * unit_rows, axis=2, keepdims=True)))
    guidance = WP * (row_grads + pooled_grad)
    return (attention, guidance)
```

```python
import functools
import math

import jax
import jax.numpy as jnp
import numpy as np
from jax import lax
from jax.experimental import pallas as pl
from jax.experimental.pallas import tpu as pltpu
from jax.sharding import PartitionSpec as P

HEADS = 32
POOL = 16
LANES = 128
MASKED = -1e30
epsilon = 1e-06
HIGH = lax.Precision.HIGHEST
NT = (((1,), (1,)), ((), ()))
NN = (((1,), (0,)), ((), ()))
MIB = 1 << 20


def mm(a, b, dims=NN, precision=None):
    return lax.dot_general(a, b, dims, precision=precision, preferred_element_type=jnp.float32)


def sinusoid(steps, embed_width):
    half_width = embed_width // 2
    frequency = jnp.exp(-math.log(10000.0) * jnp.arange(half_width, dtype=jnp.float32) / half_width)
    angles = steps.astype(jnp.float32)[:, None] * frequency[None, :]
    return jnp.concatenate([jnp.cos(angles), jnp.sin(angles)], axis=1)


def attend_kernel(block, q_ref, k_ref, v_ref, valid_ref, pool_ref, cnt_ref, *rest):
    att_ref, pooled_ref = rest[-2:]
    length = q_ref.shape[0]
    half = LANES // 2
    lane = lax.broadcasted_iota(jnp.int32, (1, LANES), 1)
    low = lane < half
    valid = valid_ref[...]
    bias = jnp.where(valid > 0.5, 0.0, MASKED)
    keys = k_ref[...]
    rows = v_ref[...]
    one = jnp.ones_like(rows)
    values = (jnp.where(low, rows, one), jnp.where(low, one, rows))

    def step(i, carry):
        at = pl.ds(pl.multiple_of(i * block, block), block)
        query = q_ref[at, :] * jnp.asarray(0.125, jnp.bfloat16)
        zero = jnp.zeros_like(query)
        outs = []
        for h in range(2):
            own = jnp.where(low, query, zero) if h == 0 else jnp.where(low, zero, query)
            scores = mm(own, keys, NT) + bias
            peak = jnp.max(scores, axis=1, keepdims=True)
            weights = jnp.exp(scores - peak).astype(jnp.bfloat16)
            outs.append(mm(weights, values[h]))
        top = jnp.where(low, outs[0], outs[1])
        total = jnp.where(low, pltpu.roll(outs[0], half, 1), pltpu.roll(outs[1], half, 1))
        mixed = ((top / total).T * valid_ref[:, at]).astype(jnp.bfloat16)
        att_ref[0, :, at] = mixed[:half]
        att_ref[1, :, at] = mixed[half:]
        return carry

    lax.fori_loop(0, length // block, step, 0)
    both = jnp.concatenate([att_ref[0], att_ref[1]], axis=0)
    pooled_ref[...] = (mm(pool_ref[...], both, NT) / cnt_ref[...]).astype(jnp.bfloat16)


def attend(qkv, valid, pool, cnt, first, count, pairs, before):
    length = qkv.shape[0]
    windows = pool.shape[0]
    head_dim = LANES // 2

    def part(which):
        return pl.BlockSpec((length, LANES), lambda j: (0, which * count + j))

    def whole(shape):
        return pl.BlockSpec(shape, lambda j: (0, 0))

    in_specs = [
        part(0),
        part(1),
        part(2),
        whole((1, length)),
        whole((windows, length)),
        whole((windows, LANES)),
    ]
    operands = [qkv, qkv, qkv, valid, pool, cnt]
    aliases = {}
    if before is not None:
        in_specs.append(pl.BlockSpec(memory_space=pl.ANY))
        operands.append(before)
        aliases = {6: 0}
    return pl.pallas_call(
        functools.partial(attend_kernel, min(512, length)),
        grid=(count,),
        out_shape=(
            jax.ShapeDtypeStruct((pairs, head_dim, length), jnp.bfloat16),
            jax.ShapeDtypeStruct((windows, count * LANES), jnp.bfloat16),
        ),
        in_specs=in_specs,
        out_specs=(
            pl.BlockSpec((2, head_dim, length), lambda j: (first + j, 0, 0)),
            pl.BlockSpec((windows, LANES), lambda j: (0, j)),
        ),
        input_output_aliases=aliases,
        compiler_params=pltpu.CompilerParams(vmem_limit_bytes=40 * MIB),
        cost_estimate=pl.CostEstimate(
            flops=count * 2 * 4 * length * length * head_dim,
            bytes_accessed=count * length * LANES * 8,
            transcendentals=count * 2 * length * length,
        ),
        name="attend",
    )(*operands)


def forward_kernel(
    lanes, own_ref, *refs
):
    n = len(lanes)
    x_refs, refs = refs[:n], refs[n:]
    (
        perm_ref, gain_ref, scale_ref, shift_ref, gate_ref, up_ref, dc_ref, cnt_ref, own_cnt_ref,
        coef_ref, class_ref, logits_ref, ga_ref, aa_ref, own_x_ref, gathered, normed,
    ) = refs
    step = pl.program_id(0)
    showers = logits_ref.shape[0]
    group = x_refs[0].shape[0] // showers
    rows = x_refs[0].shape[1]
    width = gain_ref.shape[1]
    block = own_x_ref.shape[0]
    total = rows * showers

    @pl.when(step == 0)
    def _():
        for s in range(showers):
            for m in range(group):
                at = m * (width // group)
                for ref, size in zip(x_refs, lanes):
                    gathered[s * rows : (s + 1) * rows, at : at + size] = ref[s * group + m].astype(
                        jnp.float32
                    )
                    at += size
        packed = gathered[...].astype(jnp.bfloat16)
        gathered[...] = mm(perm_ref[...], packed)
        for b in range(total // block):
            at = slice(b * block, (b + 1) * block)
            x = gathered[at]
            inverse = lax.rsqrt(jnp.mean(x * x, axis=1, keepdims=True) + epsilon)
            normed[at] = (x * inverse * gain_ref[...] * scale_ref[...] + shift_ref[...]).astype(
                jnp.bfloat16
            )
        own_x_ref[...] = gathered[pl.ds(pl.multiple_of(own_ref[0] * block, block), block), :]
        sums = mm(own_cnt_ref[...], gathered[...].astype(jnp.bfloat16))
        logits_ref[...] = mm(sums, class_ref[...].astype(jnp.float32), precision=HIGH)

    gate = mm(normed[...], gate_ref[0])
    up = mm(normed[...], up_ref[0])
    sigma = jax.nn.sigmoid(gate)
    activated = gate * sigma
    hidden = (activated * up).astype(jnp.bfloat16)
    logits_ref[...] += mm(mm(cnt_ref[...], hidden), dc_ref[0], precision=HIGH)
    coef = coef_ref[...][:, :1]
    ga_ref[0] = coef * (up * sigma * (1.0 + gate * (1.0 - sigma)))
    aa_ref[0] = coef * activated


def backward_kernel(
    parts_ref, counts_ref, bias_ref, target_ref, spread_ref, gate_ref, up_ref, dc_ref, ga_ref, aa_ref,
    dn_ref, miss_ref, total,
):
    step = pl.program_id(0)
    blocks, block, _ = dn_ref.shape

    @pl.when(step == 0)
    def _():
        logits = jnp.sum(parts_ref[...], axis=0) / counts_ref[...] + bias_ref[...]
        exponent = jnp.exp(logits - jnp.max(logits, axis=1, keepdims=True))
        miss_ref[...] = target_ref[...] - exponent / jnp.sum(exponent, axis=1, keepdims=True)

    wide = mm(mm(spread_ref[...], miss_ref[...], precision=HIGH), dc_ref[0], NT, HIGH)
    wide = jnp.concatenate([wide] * blocks, axis=0)
    gate_grad = (wide * ga_ref[0]).astype(jnp.bfloat16)
    up_grad = (wide * aa_ref[0]).astype(jnp.bfloat16)
    term = mm(gate_grad, gate_ref[0], NT) + mm(up_grad, up_ref[0], NT)

    @pl.when(step == 0)
    def _():
        total[...] = term

    @pl.when(step > 0)
    def _():
        total[...] += term

    @pl.when(step == pl.num_programs(0) - 1)
    def _():
        for b in range(blocks):
            dn_ref[b] = total[b * block : (b + 1) * block].astype(jnp.bfloat16)


def final_kernel(windows, dn_ref, x_ref, gain_ref, scale_ref, dy_ref, out_ref):
    total = dn_ref[0].astype(jnp.float32)
    for b in range(1, dn_ref.shape[0]):
        total = total + dn_ref[b].astype(jnp.float32)
    x = x_ref[...]
    inverse = lax.rsqrt(jnp.mean(x * x, axis=1, keepdims=True) + epsilon)
    unit = x * inverse
    grad = total * gain_ref[...] * scale_ref[...]
    back = inverse * (grad - unit * jnp.mean(grad * unit, axis=1, keepdims=True))
    value = windows * (dy_ref[...] + back)
    each = out_ref.shape[1]
    for s in range(out_ref.shape[0]):
        out_ref[s] = value[s * each : (s + 1) * each]


def body(
    queries,
    keys,
    values,
    slot_positions,
    counts,
    timesteps,
    labels,
    time_weight,
    norm_gain,
    gate_weight,
    up_weight,
    down_weight,
    class_weight,
    class_bias,
):
    devices = lax.axis_size("head")
    me = lax.axis_index("head")
    showers, local, width = queries.shape
    length = local * devices
    group = devices // showers
    outer = devices // group
    features = width // group
    slabs = features // LANES
    each = local // POOL
    windows = length // POOL
    classes = class_weight.shape[1]
    owned = me // group
    rows = outer * each
    block = showers * each
    total = showers * rows

    def swap(x, bit):
        return lax.ppermute(x, "head", [(d, d ^ bit) for d in range(devices)])

    chunks = [(0, slabs - 1), (slabs - 1, 1)] if slabs > 1 else [(0, 1)]

    def outgoing(x, first, count):
        x = x.reshape(showers, local, group, features)[
            ..., first * LANES : (first + count) * LANES
        ]
        return x.transpose(0, 2, 1, 3).reshape(devices, local, count * LANES)

    received = []
    for first, count in chunks:
        sent = jnp.concatenate([outgoing(x, first, count) for x in (queries, keys, values)], axis=2)
        got = lax.all_to_all(sent, "head", 0, 0, tiled=True)
        received.append(got.reshape(length, 3 * count * LANES))

    flags = (slot_positions < counts[:, None]).astype(jnp.bfloat16)
    flags = jnp.where(
        jnp.arange(devices)[:, None, None] == me, flags[None], jnp.zeros((), jnp.bfloat16)
    )
    bit = 1
    while bit < devices:
        flags = flags + swap(flags, bit)
        bit *= 2
    flags = flags.astype(jnp.float32)
    cnt = jnp.sum(flags.reshape(devices, showers, each, POOL), axis=3)
    own_flags = lax.dynamic_index_in_dim(flags, owned, 1, False).reshape(1, length)

    order = np.arange(windows).reshape(outer, group, each).transpose(1, 0, 2).reshape(windows)
    pool = jnp.asarray(order, jnp.int32)[:, None] == jnp.arange(length, dtype=jnp.int32)[None] // POOL
    pool = pool.astype(jnp.bfloat16)
    own_cnt = lax.dynamic_index_in_dim(cnt, owned, 1, False)
    own_cnt = own_cnt.reshape(outer, group, each).transpose(1, 0, 2).reshape(windows, 1)
    own_cnt = jnp.broadcast_to(jnp.maximum(own_cnt, 1.0), (windows, LANES))

    def gather(x):
        x = x[None]
        bit = 1
        while bit < group:
            x = jnp.concatenate([x, swap(x, bit)], axis=0)
            bit *= 2
        return x

    gates = gather(gate_weight)
    ups = gather(up_weight)
    class_map = gather(jnp.dot(down_weight, class_weight, preferred_element_type=jnp.float32))

    shower_counts = counts.astype(jnp.float32)
    mine = lax.dynamic_index_in_dim(
        cnt.reshape(outer, group, showers, each), me % group, 1, False
    )
    coef = (mine / shower_counts[None, :, None]).reshape(total, 1)
    coef = jnp.broadcast_to(coef, (total, LANES))
    row_shower = np.tile(np.repeat(np.arange(showers), each), outer)
    row_outer = np.repeat(np.arange(outer), block)
    cnt_rows = jnp.where(
        jnp.arange(showers)[:, None] == jnp.asarray(row_shower)[None], mine.reshape(1, total), 0.0
    )
    own_cnt_rows = jnp.where(jnp.asarray(row_outer)[None] == owned, cnt_rows, 0.0)
    source = np.arange(total).reshape(showers, outer, each).transpose(1, 0, 2).reshape(total)
    perm = jnp.asarray(source, jnp.int32)[:, None] == jnp.arange(total, dtype=jnp.int32)[None]
    perm = perm.astype(jnp.bfloat16)
    embedding = sinusoid(timesteps, time_weight.shape[0]).astype(jnp.bfloat16)
    modulation = jnp.dot(embedding, time_weight, preferred_element_type=jnp.float32)
    shifts = jnp.repeat(modulation[:, :width], each, axis=0)
    scales = jnp.repeat(1.0 + modulation[:, width:], each, axis=0)
    gain = norm_gain.reshape(1, width)

    attention = None
    pooled = []
    for qkv, (first, count) in zip(received, chunks):
        attention, part = attend(
            qkv, own_flags, pool, own_cnt, first, count, 2 * slabs, attention
        )
        part = part.reshape(1, group, rows, count * LANES)
        part = jnp.broadcast_to(part, (outer,) + part.shape[1:])
        part = part.reshape(devices, rows, count * LANES)
        pooled.append(lax.all_to_all(part, "head", 0, 0, tiled=True))

    units = gate_weight.shape[1]

    def whole(x):
        return pl.BlockSpec(x.shape, lambda i: (0,) * x.ndim)

    def member(x):
        return pl.BlockSpec((1,) + x.shape[1:], lambda i: (i, 0, 0))

    side = jax.ShapeDtypeStruct((group, total, units), jnp.float32)
    side_spec = pl.BlockSpec((1, total, units), lambda i: (i, 0, 0))
    fixed = (perm, gain, scales, shifts)
    streamed = (gates, ups, class_map)
    late = (cnt_rows.astype(jnp.bfloat16), own_cnt_rows.astype(jnp.bfloat16), coef, class_weight)
    partial, gate_side, up_side, own_x = pl.pallas_call(
        functools.partial(forward_kernel, [count * LANES for _, count in chunks]),
        grid=(group,),
        out_shape=(
            jax.ShapeDtypeStruct((showers, classes), jnp.float32),
            side,
            side,
            jax.ShapeDtypeStruct((block, width), jnp.float32),
        ),
        in_specs=[pl.BlockSpec(memory_space=pltpu.SMEM)]
        + [whole(x) for x in pooled]
        + [whole(x) for x in fixed]
        + [member(x) for x in streamed]
        + [whole(x) for x in late],
        out_specs=(
            pl.BlockSpec((showers, classes), lambda i: (0, 0)),
            side_spec,
            side_spec,
            pl.BlockSpec((block, width), lambda i: (0, 0)),
        ),
        scratch_shapes=[
            pltpu.VMEM((total, width), jnp.float32),
            pltpu.VMEM((total, width), jnp.bfloat16),
        ],
        compiler_params=pltpu.CompilerParams(vmem_limit_bytes=40 * MIB),
        name="classifier_forward",
    )(owned.reshape(1).astype(jnp.int32), *pooled, *fixed, *streamed, *late)

    parts = lax.all_to_all(
        jnp.broadcast_to(partial[None], (devices,) + partial.shape), "head", 0, 0, tiled=True
    )
    target = (labels[:, None] == jnp.arange(classes, dtype=jnp.int32)[None]).astype(jnp.float32)
    spread = jnp.asarray(
        np.repeat(np.eye(showers), each, axis=0).astype(np.float32)
    )
    heads_in = (
        parts,
        jnp.broadcast_to(shower_counts[:, None], (showers, classes)),
        class_bias.reshape(1, classes),
        target,
        spread,
    )
    grads, miss = pl.pallas_call(
        backward_kernel,
        grid=(group,),
        out_shape=(
            jax.ShapeDtypeStruct((outer, block, width), jnp.bfloat16),
            jax.ShapeDtypeStruct((showers, classes), jnp.float32),
        ),
        in_specs=[whole(x) for x in heads_in]
        + [member(x) for x in streamed + (gate_side, up_side)],
        out_specs=(
            pl.BlockSpec((outer, block, width), lambda i: (0, 0, 0)),
            pl.BlockSpec((showers, classes), lambda i: (0, 0)),
        ),
        scratch_shapes=[pltpu.VMEM((total, width), jnp.float32)],
        compiler_params=pltpu.CompilerParams(vmem_limit_bytes=40 * MIB),
        name="classifier_backward",
    )(*heads_in, *streamed, gate_side, up_side)

    lines = [[o * group + m for o in range(outer)] for m in range(group)]
    grads = lax.all_to_all(grads, "head", 0, 0, axis_index_groups=lines, tiled=True)
    feature_grad = mm(miss, class_weight.astype(jnp.float32), NT, HIGH)
    here = lax.dynamic_index_in_dim(cnt, me, 0, False)
    own_row_grads = (here / shower_counts[:, None])[:, :, None] * feature_grad[:, None, :]
    own_row_grads = own_row_grads.reshape(block, width)
    guidance = pl.pallas_call(
        functools.partial(final_kernel, float(windows)),
        out_shape=jax.ShapeDtypeStruct((showers, each, width), jnp.float32),
        compiler_params=pltpu.CompilerParams(vmem_limit_bytes=40 * MIB),
        name="norm_backward",
    )(grads, own_x, gain, scales, own_row_grads)
    return (attention.transpose(0, 2, 1), guidance)


def solution(mesh):
    in_specs = (
        P("parts", "head", None),
        P("parts", "head", None),
        P("parts", "head", None),
        P("parts", "head"),
        P("parts"),
        P("parts"),
        P("parts"),
        P(),
        P(),
        P(None, "head"),
        P(None, "head"),
        P("head", None),
        P(),
        P(),
    )
    out_specs = (P(("parts", "head"), None, None), P("parts", "head", None))
    return jax.shard_map(body, mesh=mesh, in_specs=in_specs, out_specs=out_specs, check_vma=False)
```

```python
import functools
import math

import jax
import jax.numpy as jnp
import numpy as np
from jax import lax
from jax.experimental import pallas as pl
from jax.experimental.pallas import tpu as pltpu
from jax.sharding import PartitionSpec as P

HEADS = 32
POOL = 16
LANES = 128
MASKED = -1e30
ABSENT = 64.0
epsilon = 1e-06
HIGH = lax.Precision.HIGHEST
NT = (((1,), (1,)), ((), ()))
NN = (((1,), (0,)), ((), ()))
MIB = 1 << 20


def mm(a, b, dims=NN, precision=None):
    return lax.dot_general(a, b, dims, precision=precision, preferred_element_type=jnp.float32)


def sinusoid(steps, embed_width):
    half_width = embed_width // 2
    frequency = jnp.exp(-math.log(10000.0) * jnp.arange(half_width, dtype=jnp.float32) / half_width)
    angles = steps.astype(jnp.float32)[:, None] * frequency[None, :]
    return jnp.concatenate([jnp.cos(angles), jnp.sin(angles)], axis=1)


def pack_kernel(chunks, slot_ref, count_ref, q_ref, k_ref, v_ref, *outs):
    shower = pl.program_id(0)
    group = outs[0].shape[0]
    local = q_ref.shape[1]
    features = q_ref.shape[2] // group
    valid = (slot_ref[pl.ds(shower, 1), :] < count_ref[shower]).astype(jnp.float32)
    square = (local, local)
    diagonal = lax.broadcasted_iota(jnp.int32, square, 0) == lax.broadcasted_iota(
        jnp.int32, square, 1
    )
    column = jnp.sum(jnp.where(diagonal, valid, 0.0), axis=1, keepdims=True) > 0.5
    for (first, count), out in zip(chunks, outs):
        size = count * LANES
        for m in range(group):
            at = m * features + first * LANES
            for t, ref in enumerate((q_ref, k_ref, v_ref)):
                part = ref[0, :, at : at + size]
                if t == 1:
                    part = jnp.where(column, part, jnp.asarray(ABSENT, part.dtype))
                out[m, :, t * size : (t + 1) * size] = part


def attend_kernel(block, q_ref, k_ref, v_ref, pool_ref, *rest):
    att_ref, pooled_ref = rest[-2:]
    length = q_ref.shape[0]
    half = LANES // 2
    lane = lax.broadcasted_iota(jnp.int32, (1, LANES), 1)
    low = lane < half
    keys = k_ref[...]
    rows = v_ref[...]
    one = jnp.ones_like(rows)
    present = jnp.where(keys.astype(jnp.float32) < 0.5 * ABSENT, 1.0, 0.0).astype(jnp.bfloat16)
    pick = jnp.broadcast_to(jnp.where(lane == 0, 1.0, 0.0).astype(jnp.bfloat16), (8, LANES))
    valid = mm(pick, present, NT)[:1]
    bias = jnp.where(valid > 0.5, 0.0, MASKED)
    values = (jnp.where(low, rows, one), jnp.where(low, one, rows))

    for i in range(length // block):
        at = slice(i * block, (i + 1) * block)
        query = q_ref[at, :] * jnp.asarray(0.125, jnp.bfloat16)
        zero = jnp.zeros_like(query)
        outs = []
        for h in range(2):
            own = jnp.where(low, query, zero) if h == 0 else jnp.where(low, zero, query)
            scores = mm(own, keys, NT) + bias
            peak = jnp.max(scores, axis=1, keepdims=True)
            weights = jnp.exp(scores - peak).astype(jnp.bfloat16)
            outs.append(mm(weights, values[h]))
        top = jnp.where(low, outs[0], outs[1])
        total = jnp.where(low, pltpu.roll(outs[0], half, 1), pltpu.roll(outs[1], half, 1))
        mixed = ((top / total).T * valid[:, at]).astype(jnp.bfloat16)
        att_ref[0, :, at] = mixed[:half]
        att_ref[1, :, at] = mixed[half:]
    both = jnp.concatenate([att_ref[0], att_ref[1]], axis=0)
    cnt = mm(pool_ref[...], jnp.broadcast_to(valid, (LANES, length)).astype(jnp.bfloat16), NT)
    pooled = (mm(pool_ref[...], both, NT) / jnp.maximum(cnt, 1.0)).astype(jnp.bfloat16)
    rows = pooled_ref.shape[1]
    group = pooled.shape[0] // rows
    for d in range(pooled_ref.shape[0]):
        m = d % group
        pooled_ref[d] = pooled[m * rows : (m + 1) * rows]


def attend(qkv, pool, first, count, pairs, devices, rows, before):
    length = qkv.shape[0]
    windows = pool.shape[0]
    head_dim = LANES // 2

    def part(which):
        return pl.BlockSpec((length, LANES), lambda j: (0, which * count + j))

    def whole(shape):
        return pl.BlockSpec(shape, lambda j: (0, 0))

    in_specs = [
        part(0),
        part(1),
        part(2),
        whole((windows, length)),
    ]
    operands = [qkv, qkv, qkv, pool]
    aliases = {}
    if before is not None:
        in_specs.append(pl.BlockSpec(memory_space=pl.ANY))
        operands.append(before)
        aliases = {4: 0}
    return pl.pallas_call(
        functools.partial(attend_kernel, min(512, length)),
        grid=(count,),
        out_shape=(
            jax.ShapeDtypeStruct((pairs, head_dim, length), jnp.bfloat16),
            jax.ShapeDtypeStruct((devices, rows, count * LANES), jnp.bfloat16),
        ),
        in_specs=in_specs,
        out_specs=(
            pl.BlockSpec((2, head_dim, length), lambda j: (first + j, 0, 0)),
            pl.BlockSpec((devices, rows, LANES), lambda j: (0, 0, j)),
        ),
        input_output_aliases=aliases,
        compiler_params=pltpu.CompilerParams(vmem_limit_bytes=40 * MIB),
        cost_estimate=pl.CostEstimate(
            flops=count * 2 * 4 * length * length * head_dim,
            bytes_accessed=count * length * LANES * 8,
            transcendentals=count * 2 * length * length,
        ),
        name="attend",
    )(*operands)


def forward_kernel(
    lanes, own_ref, *refs
):
    n = len(lanes)
    x_refs, refs = refs[:n], refs[n:]
    (
        perm_ref, gain_ref, scale_ref, shift_ref, gate_ref, up_ref, dc_ref, cnt_ref, own_cnt_ref,
        coef_ref, class_ref, copies_ref, ga_ref, aa_ref, own_x_ref, gathered, normed, logits_ref,
    ) = refs
    step = pl.program_id(0)
    showers = logits_ref.shape[0]
    group = x_refs[0].shape[0] // showers
    rows = x_refs[0].shape[1]
    width = gain_ref.shape[1]
    block = own_x_ref.shape[0]
    total = rows * showers

    @pl.when(step == 0)
    def _():
        for s in range(showers):
            for m in range(group):
                at = m * (width // group)
                for ref, size in zip(x_refs, lanes):
                    gathered[s * rows : (s + 1) * rows, at : at + size] = ref[s * group + m].astype(
                        jnp.float32
                    )
                    at += size
        packed = gathered[...].astype(jnp.bfloat16)
        gathered[...] = mm(perm_ref[...], packed)
        for b in range(total // block):
            at = slice(b * block, (b + 1) * block)
            x = gathered[at]
            inverse = lax.rsqrt(jnp.mean(x * x, axis=1, keepdims=True) + epsilon)
            normed[at] = (x * inverse * gain_ref[...] * scale_ref[...] + shift_ref[...]).astype(
                jnp.bfloat16
            )
        own_x_ref[...] = gathered[pl.ds(pl.multiple_of(own_ref[0] * block, block), block), :]
        sums = mm(own_cnt_ref[...], gathered[...].astype(jnp.bfloat16))
        logits_ref[...] = mm(sums, class_ref[...].astype(jnp.float32), precision=HIGH)

    gate = mm(normed[...], gate_ref[0])
    up = mm(normed[...], up_ref[0])
    sigma = jax.nn.sigmoid(gate)
    activated = gate * sigma
    hidden = (activated * up).astype(jnp.bfloat16)
    logits_ref[...] += mm(mm(cnt_ref[...], hidden), dc_ref[0], precision=HIGH)
    coef = coef_ref[...][:, :1]
    ga_ref[0] = coef * (up * sigma * (1.0 + gate * (1.0 - sigma)))
    aa_ref[0] = coef * activated

    @pl.when(step == pl.num_programs(0) - 1)
    def _():
        for d in range(copies_ref.shape[0]):
            copies_ref[d] = logits_ref[...]


def backward_kernel(
    parts_ref, counts_ref, bias_ref, target_ref, spread_ref, gate_ref, up_ref, dc_ref, ga_ref, aa_ref,
    dn_ref, miss_ref, total,
):
    step = pl.program_id(0)
    blocks, block, _ = dn_ref.shape

    @pl.when(step == 0)
    def _():
        logits = jnp.sum(parts_ref[...], axis=0) / counts_ref[...] + bias_ref[...]
        exponent = jnp.exp(logits - jnp.max(logits, axis=1, keepdims=True))
        miss_ref[...] = target_ref[...] - exponent / jnp.sum(exponent, axis=1, keepdims=True)

    wide = mm(mm(spread_ref[...], miss_ref[...], precision=HIGH), dc_ref[0], NT, HIGH)
    wide = jnp.concatenate([wide] * blocks, axis=0)
    gate_grad = (wide * ga_ref[0]).astype(jnp.bfloat16)
    up_grad = (wide * aa_ref[0]).astype(jnp.bfloat16)
    term = mm(gate_grad, gate_ref[0], NT) + mm(up_grad, up_ref[0], NT)

    @pl.when(step == 0)
    def _():
        total[...] = term

    @pl.when(step > 0)
    def _():
        total[...] += term

    @pl.when(step == pl.num_programs(0) - 1)
    def _():
        for b in range(blocks):
            dn_ref[b] = total[b * block : (b + 1) * block].astype(jnp.bfloat16)


def final_kernel(windows, dn_ref, x_ref, gain_ref, scale_ref, dy_ref, out_ref):
    total = dn_ref[0].astype(jnp.float32)
    for b in range(1, dn_ref.shape[0]):
        total = total + dn_ref[b].astype(jnp.float32)
    x = x_ref[...]
    inverse = lax.rsqrt(jnp.mean(x * x, axis=1, keepdims=True) + epsilon)
    unit = x * inverse
    grad = total * gain_ref[...] * scale_ref[...]
    back = inverse * (grad - unit * jnp.mean(grad * unit, axis=1, keepdims=True))
    value = windows * (dy_ref[...] + back)
    each = out_ref.shape[1]
    for s in range(out_ref.shape[0]):
        out_ref[s] = value[s * each : (s + 1) * each]


def body(
    queries,
    keys,
    values,
    slot_positions,
    counts,
    timesteps,
    labels,
    time_weight,
    norm_gain,
    gate_weight,
    up_weight,
    down_weight,
    class_weight,
    class_bias,
):
    devices = lax.axis_size("head")
    me = lax.axis_index("head")
    showers, local, width = queries.shape
    length = local * devices
    group = devices // showers
    outer = devices // group
    features = width // group
    slabs = features // LANES
    each = local // POOL
    windows = length // POOL
    classes = class_weight.shape[1]
    owned = me // group
    rows = outer * each
    block = showers * each
    total = showers * rows

    def swap(x, bit):
        return lax.ppermute(x, "head", [(d, d ^ bit) for d in range(devices)])

    chunks = [(0, slabs - 1), (slabs - 1, 1)] if slabs > 1 else [(0, 1)]

    sent = pl.pallas_call(
        functools.partial(pack_kernel, chunks),
        grid=(showers,),
        out_shape=[
            jax.ShapeDtypeStruct((devices, local, 3 * count * LANES), jnp.bfloat16)
            for _, count in chunks
        ],
        in_specs=[
            pl.BlockSpec((showers, local), lambda s: (0, 0)),
            pl.BlockSpec(memory_space=pltpu.SMEM),
        ]
        + [pl.BlockSpec((1, local, width), lambda s: (s, 0, 0))] * 3,
        out_specs=[
            pl.BlockSpec((group, local, 3 * count * LANES), lambda s: (s, 0, 0))
            for _, count in chunks
        ],
        compiler_params=pltpu.CompilerParams(vmem_limit_bytes=60 * MIB),
        name="pack",
    )(slot_positions, counts, queries, keys, values)
    sent, slot_positions, gate_weight, up_weight, down_weight = lax.optimization_barrier(
        (sent, slot_positions, gate_weight, up_weight, down_weight)
    )

    def exchange(x):
        got = lax.all_to_all(x, "head", 0, 0, tiled=True)
        return got.reshape(length, x.shape[2])

    received = [exchange(sent[0])]

    valid = (slot_positions < counts[:, None]).astype(jnp.float32)
    here = jnp.sum(valid.reshape(showers, each, POOL), axis=2)
    mine = jnp.where(jnp.arange(outer)[:, None, None] == owned, here[None], 0.0)
    bit = devices // 2
    while bit >= group:
        mine = mine + swap(mine, bit)
        bit //= 2

    order = np.arange(windows).reshape(outer, group, each).transpose(1, 0, 2).reshape(windows)
    pool = jnp.asarray(order, jnp.int32)[:, None] == jnp.arange(length, dtype=jnp.int32)[None] // POOL
    pool = pool.astype(jnp.bfloat16)

    def gather(x):
        x = [x[None]]
        bit = group // 2
        while bit:
            x = [jnp.concatenate(x, axis=0)]
            x.append(swap(x[0], bit))
            bit //= 2
        return x

    gates = gather(gate_weight)
    ups = gather(up_weight)
    class_map = gather(jnp.dot(down_weight, class_weight, preferred_element_type=jnp.float32))

    sent, gates, ups, class_map, mine = lax.optimization_barrier(
        (sent[1:], gates, ups, class_map, mine)
    )
    received += [exchange(x) for x in sent]

    shower_counts = counts.astype(jnp.float32)
    coef = (mine / shower_counts[None, :, None]).reshape(total, 1)
    coef = jnp.broadcast_to(coef, (total, LANES))
    row_shower = np.tile(np.repeat(np.arange(showers), each), outer)
    row_outer = np.repeat(np.arange(outer), block)
    cnt_rows = jnp.where(
        jnp.arange(showers)[:, None] == jnp.asarray(row_shower)[None], mine.reshape(1, total), 0.0
    )
    own_cnt_rows = jnp.where(jnp.asarray(row_outer)[None] == owned, cnt_rows, 0.0)
    source = np.arange(total).reshape(showers, outer, each).transpose(1, 0, 2).reshape(total)
    perm = jnp.asarray(source, jnp.int32)[:, None] == jnp.arange(total, dtype=jnp.int32)[None]
    perm = perm.astype(jnp.bfloat16)
    embedding = sinusoid(timesteps, time_weight.shape[0]).astype(jnp.bfloat16)
    modulation = jnp.dot(embedding, time_weight, preferred_element_type=jnp.float32)
    shifts = jnp.repeat(modulation[:, :width], each, axis=0)
    scales = jnp.repeat(1.0 + modulation[:, width:], each, axis=0)
    gain = norm_gain.reshape(1, width)

    target = (labels[:, None] == jnp.arange(classes, dtype=jnp.int32)[None]).astype(jnp.float32)
    spread = jnp.asarray(
        np.repeat(np.eye(showers), each, axis=0).astype(np.float32)
    )
    spread_counts = jnp.broadcast_to(shower_counts[:, None], (showers, classes))
    heads_in = (spread_counts, class_bias.reshape(1, classes), target, spread)
    fixed = (perm, gain, scales, shifts)
    streamed = tuple(jnp.concatenate(x, axis=0) for x in (gates, ups, class_map))
    late = (cnt_rows.astype(jnp.bfloat16), own_cnt_rows.astype(jnp.bfloat16), coef, class_weight)

    attention = None
    pooled = []
    for qkv, (first, count) in zip(received, chunks):
        attention, part = attend(
            qkv, pool, first, count, 2 * slabs, devices, rows, attention
        )
        if pooled:
            part, pooled[-1] = lax.optimization_barrier((part, pooled[-1]))
        else:
            part, fixed, streamed, late, heads_in = lax.optimization_barrier(
                (part, fixed, streamed, late, heads_in)
            )
        pooled.append(lax.all_to_all(part, "head", 0, 0, tiled=True))

    units = gate_weight.shape[1]

    def whole(x):
        return pl.BlockSpec(x.shape, lambda i: (0,) * x.ndim)

    def member(x):
        return pl.BlockSpec((1,) + x.shape[1:], lambda i: (i, 0, 0))

    side = jax.ShapeDtypeStruct((group, total, units), jnp.float32)
    side_spec = pl.BlockSpec((1, total, units), lambda i: (i, 0, 0))
    partial, gate_side, up_side, own_x = pl.pallas_call(
        functools.partial(forward_kernel, [count * LANES for _, count in chunks]),
        grid=(group,),
        out_shape=(
            jax.ShapeDtypeStruct((devices, showers, classes), jnp.float32),
            side,
            side,
            jax.ShapeDtypeStruct((block, width), jnp.float32),
        ),
        in_specs=[pl.BlockSpec(memory_space=pltpu.SMEM)]
        + [whole(x) for x in pooled]
        + [whole(x) for x in fixed]
        + [member(x) for x in streamed]
        + [whole(x) for x in late],
        out_specs=(
            pl.BlockSpec((devices, showers, classes), lambda i: (0, 0, 0)),
            side_spec,
            side_spec,
            pl.BlockSpec((block, width), lambda i: (0, 0)),
        ),
        scratch_shapes=[
            pltpu.VMEM((total, width), jnp.float32),
            pltpu.VMEM((total, width), jnp.bfloat16),
            pltpu.VMEM((showers, classes), jnp.float32),
        ],
        compiler_params=pltpu.CompilerParams(vmem_limit_bytes=56 * MIB),
        name="classifier_forward",
    )(owned.reshape(1).astype(jnp.int32), *pooled, *fixed, *streamed, *late)

    parts = lax.all_to_all(partial, "head", 0, 0, tiled=True)
    grads, miss = pl.pallas_call(
        backward_kernel,
        grid=(group,),
        out_shape=(
            jax.ShapeDtypeStruct((outer, block, width), jnp.bfloat16),
            jax.ShapeDtypeStruct((showers, classes), jnp.float32),
        ),
        in_specs=[whole(x) for x in (parts,) + heads_in]
        + [member(x) for x in streamed + (gate_side, up_side)],
        out_specs=(
            pl.BlockSpec((outer, block, width), lambda i: (0, 0, 0)),
            pl.BlockSpec((showers, classes), lambda i: (0, 0)),
        ),
        scratch_shapes=[pltpu.VMEM((total, width), jnp.float32)],
        compiler_params=pltpu.CompilerParams(vmem_limit_bytes=56 * MIB),
        name="classifier_backward",
    )(parts, *heads_in, *streamed, gate_side, up_side)

    lines = [[o * group + m for o in range(outer)] for m in range(group)]
    grads = lax.all_to_all(grads, "head", 0, 0, axis_index_groups=lines, tiled=True)
    feature_grad = mm(miss, class_weight.astype(jnp.float32), NT, HIGH)
    own_row_grads = (here / shower_counts[:, None])[:, :, None] * feature_grad[:, None, :]
    own_row_grads = own_row_grads.reshape(block, width)
    guidance = pl.pallas_call(
        functools.partial(final_kernel, float(windows)),
        out_shape=jax.ShapeDtypeStruct((showers, each, width), jnp.float32),
        compiler_params=pltpu.CompilerParams(vmem_limit_bytes=40 * MIB),
        name="norm_backward",
    )(grads, own_x, gain, scales, own_row_grads)
    return (attention.transpose(0, 2, 1), guidance)


def solution(mesh):
    in_specs = (
        P("parts", "head", None),
        P("parts", "head", None),
        P("parts", "head", None),
        P("parts", "head"),
        P("parts"),
        P("parts"),
        P("parts"),
        P(),
        P(),
        P(None, "head"),
        P(None, "head"),
        P("head", None),
        P(),
        P(),
    )
    out_specs = (P(("parts", "head"), None, None), P("parts", "head", None))
    return jax.shard_map(body, mesh=mesh, in_specs=in_specs, out_specs=out_specs, check_vma=False)
```

```python
import functools
import math

import jax
import jax.numpy as jnp
import numpy as np
from jax import lax
from jax.experimental import pallas as pl
from jax.experimental.pallas import tpu as pltpu
from jax.sharding import PartitionSpec as P

HEADS = 32
POOL = 16
LANES = 128
MASKED = -1e30
HEAD = 16
TEAMS = 8
ABSENT = 64.0
epsilon = 1e-06
HIGH = lax.Precision.HIGHEST
NT = (((1,), (1,)), ((), ()))
TN = (((0,), (0,)), ((), ()))
NN = (((1,), (0,)), ((), ()))
MIB = 1 << 20


def mm(a, b, dims=NN, precision=None):
    return lax.dot_general(a, b, dims, precision=precision, preferred_element_type=jnp.float32)


def sinusoid(steps, embed_width):
    half_width = embed_width // 2
    frequency = jnp.exp(-math.log(10000.0) * jnp.arange(half_width, dtype=jnp.float32) / half_width)
    angles = steps.astype(jnp.float32)[:, None] * frequency[None, :]
    return jnp.concatenate([jnp.cos(angles), jnp.sin(angles)], axis=1)


def pack_kernel(first, count, slot_ref, count_ref, q_ref, k_ref, v_ref, out):
    shower = pl.program_id(0)
    group = out.shape[0]
    local = q_ref.shape[1]
    features = q_ref.shape[2] // group
    size = count * LANES
    valid = (slot_ref[pl.ds(shower, 1), :] < count_ref[shower]).astype(jnp.float32)
    square = (local, local)
    diagonal = lax.broadcasted_iota(jnp.int32, square, 0) == lax.broadcasted_iota(
        jnp.int32, square, 1
    )
    column = jnp.sum(jnp.where(diagonal, valid, 0.0), axis=1, keepdims=True) > 0.5
    for m in range(group):
        at = m * features + first * LANES
        for t, ref in enumerate((q_ref, k_ref, v_ref)):
            part = ref[0, :, at : at + size]
            if t == 1:
                part = jnp.where(column, part, jnp.asarray(ABSENT, part.dtype))
            out[m, :, t * size : (t + 1) * size] = part


def pack(slot_positions, counts, queries, keys, values, first, count, devices):
    showers, local, width = queries.shape
    group = devices // showers
    return pl.pallas_call(
        functools.partial(pack_kernel, first, count),
        grid=(showers,),
        out_shape=jax.ShapeDtypeStruct((devices, local, 3 * count * LANES), jnp.bfloat16),
        in_specs=[
            pl.BlockSpec((showers, local), lambda s: (0, 0)),
            pl.BlockSpec(memory_space=pltpu.SMEM),
        ]
        + [pl.BlockSpec((1, local, width), lambda s: (s, 0, 0))] * 3,
        out_specs=pl.BlockSpec((group, local, 3 * count * LANES), lambda s: (s, 0, 0)),
        compiler_params=pltpu.CompilerParams(vmem_limit_bytes=58 * MIB),
        name="pack",
    )(slot_positions, counts, queries, keys, values)


def attend_kernel(block, head, q_ref, k_ref, v_ref, pool_ref, *rest):
    att_ref, pooled_ref = rest[-2:]
    length = q_ref.shape[0]
    half = LANES // 2
    lane = lax.broadcasted_iota(jnp.int32, (1, LANES), 1)
    low = lane < half
    keys = k_ref[...]
    rows = v_ref[...]
    one = jnp.ones_like(rows)
    present = jnp.where(keys.astype(jnp.float32) < 0.5 * ABSENT, 1.0, 0.0).astype(jnp.bfloat16)
    pick = jnp.broadcast_to(jnp.where(lane == 0, 1.0, 0.0).astype(jnp.bfloat16), (8, LANES))
    valid = mm(pick, present, NT)[:1]
    bias = jnp.where(valid > 0.5, 0.0, MASKED)
    values = (jnp.where(low, rows, one), jnp.where(low, one, rows))

    for i in range(length // block):
        at = slice(i * block, (i + 1) * block)
        query = q_ref[at, :] * jnp.asarray(0.125, jnp.bfloat16)
        zero = jnp.zeros_like(query)
        outs = []
        for h in range(2):
            own = jnp.where(low, query, zero) if h == 0 else jnp.where(low, zero, query)
            scores = mm(own, keys, NT) + bias
            peak = jnp.max(scores, axis=1, keepdims=True)
            weights = jnp.exp(scores - peak).astype(jnp.bfloat16)
            outs.append(mm(weights, values[h]))
        top = jnp.where(low, outs[0], outs[1])
        total = jnp.where(low, pltpu.roll(outs[0], half, 1), pltpu.roll(outs[1], half, 1))
        mixed = ((top / total).T * valid[:, at]).astype(jnp.bfloat16)
        att_ref[0, :, at] = mixed[:half]
        att_ref[1, :, at] = mixed[half:]
    both = jnp.concatenate([att_ref[0], att_ref[1]], axis=0)
    cnt = mm(pool_ref[...], jnp.broadcast_to(valid, (LANES, length)).astype(jnp.bfloat16), NT)
    pooled = (mm(pool_ref[...], both, NT) / jnp.maximum(cnt, 1.0)).astype(jnp.bfloat16)
    rows = pooled_ref.shape[1] - head
    team = pooled.shape[0] // rows
    if head:
        ones = jnp.broadcast_to(valid, (head, length)).astype(jnp.bfloat16)
        counted = mm(ones, pool_ref[...], NT).astype(jnp.bfloat16)
    for d in range(pooled_ref.shape[0]):
        m = d % team
        pooled_ref[d, head:] = pooled[m * rows : (m + 1) * rows]
        if head:
            pooled_ref[d, :head] = counted


def attend(qkv, pool, first, count, pairs, devices, rows, head, before):
    length = qkv.shape[0]
    windows = pool.shape[0]
    head_dim = LANES // 2

    def part(which):
        return pl.BlockSpec((length, LANES), lambda j: (0, which * count + j))

    def whole(shape):
        return pl.BlockSpec(shape, lambda j: (0, 0))

    in_specs = [
        part(0),
        part(1),
        part(2),
        whole((windows, length)),
    ]
    operands = [qkv, qkv, qkv, pool]
    aliases = {}
    if before is not None:
        in_specs.append(pl.BlockSpec(memory_space=pl.ANY))
        operands.append(before)
        aliases = {4: 0}
    return pl.pallas_call(
        functools.partial(attend_kernel, min(512, length), head),
        grid=(count,),
        out_shape=(
            jax.ShapeDtypeStruct((pairs, head_dim, length), jnp.bfloat16),
            jax.ShapeDtypeStruct((devices, head + rows, count * LANES), jnp.bfloat16),
        ),
        in_specs=in_specs,
        out_specs=(
            pl.BlockSpec((2, head_dim, length), lambda j: (first + j, 0, 0)),
            pl.BlockSpec((devices, head + rows, LANES), lambda j: (0, 0, j)),
        ),
        input_output_aliases=aliases,
        compiler_params=pltpu.CompilerParams(vmem_limit_bytes=40 * MIB),
        cost_estimate=pl.CostEstimate(
            flops=count * 2 * 4 * length * length * head_dim,
            bytes_accessed=count * length * LANES * 8,
            transcendentals=count * 2 * length * length,
        ),
        name="attend",
    )(*operands)


def forward_kernel(lanes, team, rows, place_ref, *refs):
    n = len(lanes)
    inputs = n + 6 + 3 * team
    sources, (copies_ref, ga_out, aa_out, own_x_ref) = refs[:inputs], refs[inputs : inputs + 4]
    buffers = refs[inputs + 4 : 2 * inputs + 4]
    gathered, normed, counted, ga_ref, aa_ref, sems, out_sems = refs[2 * inputs + 4 :]
    arriving = [
        pltpu.make_async_copy(source, buffer, sems.at[i])
        for i, (source, buffer) in enumerate(zip(sources, buffers))
    ]
    for copy in arriving:
        copy.start()

    def get(i):
        arriving[i].wait()
        return buffers[i]

    showers = copies_ref.shape[1]
    group = buffers[0].shape[0] // showers
    width = gathered.shape[1]
    block = own_x_ref.shape[0]
    total = rows * showers
    x_refs = [get(i) for i in range(n)]
    for s in range(showers):
        for m in range(group):
            at = m * (width // group)
            for ref, size in zip(x_refs, lanes):
                part = ref[s * group + m, ref.shape[1] - rows :]
                gathered[s * rows : (s + 1) * rows, at : at + size] = part.astype(jnp.float32)
                at += size
    packed = gathered[...].astype(jnp.bfloat16)
    perm_ref, gain_ref, scale_ref, shift_ref = [get(n + i) for i in range(4)]
    gathered[...] = mm(perm_ref[...], packed)
    for b in range(total // block):
        at = slice(b * block, (b + 1) * block)
        x = gathered[at]
        inverse = lax.rsqrt(jnp.mean(x * x, axis=1, keepdims=True) + epsilon)
        normed[at] = (x * inverse * gain_ref[...] * scale_ref[...] + shift_ref[...]).astype(
            jnp.bfloat16
        )
    own_x_ref[...] = gathered[pl.ds(pl.multiple_of(place_ref[0] * block, block), block), :]
    counts_ref, class_ref = [get(n + 4 + i) for i in range(2)]
    counted[...] = jnp.zeros(counted.shape, jnp.float32)
    for s in range(showers):
        counted[s : s + 1] = x_refs[-1][s * group, :HEAD].astype(jnp.float32)[:1]
    shape = (total, LANES)
    row = lax.broadcasted_iota(jnp.int32, shape, 0)
    lane = lax.broadcasted_iota(jnp.int32, shape, 1)
    each = block // showers
    from_lane = place_ref[1] * rows + row // block * each + row % each
    pick = jnp.where(lane == from_lane, 1.0, 0.0).astype(jnp.bfloat16)
    cnt_of = mm(pick, counted[...].astype(jnp.bfloat16), NT)
    cnt_of = jnp.where(lane == row % block // each, cnt_of, 0.0)
    cnt = jnp.sum(cnt_of, axis=1, keepdims=True)
    own_cnt_of = jnp.where(row // block == place_ref[0], cnt_of, 0.0).astype(jnp.bfloat16)
    cnt_of = cnt_of.astype(jnp.bfloat16)
    sums = mm(own_cnt_of, gathered[...].astype(jnp.bfloat16), TN)[:showers]
    logits = mm(sums, class_ref[...].astype(jnp.float32), precision=HIGH)
    coef = cnt / counts_ref[...][:, :1]
    leaving = []
    for i in range(team):
        gate_ref, up_ref, map_ref = [get(n + 6 + 3 * i + j) for j in range(3)]
        gate = mm(normed[...], gate_ref[...])
        up = mm(normed[...], up_ref[...])
        sigma = jax.nn.sigmoid(gate)
        activated = gate * sigma
        hidden = (activated * up).astype(jnp.bfloat16)
        logits = logits + mm(mm(cnt_of, hidden, TN)[:showers], map_ref[...], precision=HIGH)
        ga_ref[i] = coef * (up * sigma * (1.0 + gate * (1.0 - sigma)))
        aa_ref[i] = coef * activated
        for j, (kept, out) in enumerate(((ga_ref, ga_out), (aa_ref, aa_out))):
            copy = pltpu.make_async_copy(kept.at[i], out.at[i], out_sems.at[2 * i + j])
            copy.start()
            leaving.append(copy)
    for d in range(copies_ref.shape[0]):
        copies_ref[d] = logits
    for copy in leaving:
        copy.wait()


def backward_kernel(team, parts_ref, counts_ref, bias_ref, target_ref, spread_ref, *refs):
    sources = refs[: 3 * team]
    ga_in, aa_in, dn_ref, miss_ref = refs[3 * team : 3 * team + 4]
    buffers = refs[3 * team + 4 : 6 * team + 4]
    ga_ref, aa_ref, total, sems = refs[6 * team + 4 :]
    arriving = []
    for i in range(team):
        pairs = [(sources[3 * i + 2], buffers[3 * i + 2]), (ga_in.at[i], ga_ref.at[i])]
        pairs += [(aa_in.at[i], aa_ref.at[i])]
        pairs += [(sources[3 * i + j], buffers[3 * i + j]) for j in range(2)]
        arriving.append(
            [
                pltpu.make_async_copy(source, buffer, sems.at[5 * i + j])
                for j, (source, buffer) in enumerate(pairs)
            ]
        )
        for copy in arriving[-1]:
            copy.start()
    blocks, block, _ = dn_ref.shape
    logits = jnp.sum(parts_ref[...], axis=0) / counts_ref[...] + bias_ref[...]
    exponent = jnp.exp(logits - jnp.max(logits, axis=1, keepdims=True))
    miss = target_ref[...] - exponent / jnp.sum(exponent, axis=1, keepdims=True)
    miss_ref[...] = miss
    spread = mm(spread_ref[...], miss, precision=HIGH)
    for i in range(team):
        gate_ref, up_ref, map_ref = buffers[3 * i : 3 * i + 3]
        for copy in arriving[i]:
            copy.wait()
        wide = mm(spread, map_ref[...], NT, HIGH)
        wide = jnp.concatenate([wide] * blocks, axis=0)
        gate_grad = (wide * ga_ref[i]).astype(jnp.bfloat16)
        up_grad = (wide * aa_ref[i]).astype(jnp.bfloat16)
        term = mm(gate_grad, gate_ref[...], NT) + mm(up_grad, up_ref[...], NT)
        if i == 0:
            total[...] = term
        elif i < team - 1:
            total[...] += term
        else:
            term = (total[...] + term).astype(jnp.bfloat16)
            for b in range(blocks):
                dn_ref[b] = term[b * block : (b + 1) * block]


def final_kernel(windows, dn_ref, x_ref, gain_ref, scale_ref, dy_ref, out_ref):
    total = dn_ref[0].astype(jnp.float32)
    for b in range(1, dn_ref.shape[0]):
        total = total + dn_ref[b].astype(jnp.float32)
    x = x_ref[...]
    inverse = lax.rsqrt(jnp.mean(x * x, axis=1, keepdims=True) + epsilon)
    unit = x * inverse
    grad = total * gain_ref[...] * scale_ref[...]
    back = inverse * (grad - unit * jnp.mean(grad * unit, axis=1, keepdims=True))
    value = windows * (dy_ref[...] + back)
    each = out_ref.shape[1]
    for s in range(out_ref.shape[0]):
        out_ref[s] = value[s * each : (s + 1) * each]


def body(
    queries,
    keys,
    values,
    slot_positions,
    counts,
    timesteps,
    labels,
    time_weight,
    norm_gain,
    gate_weight,
    up_weight,
    down_weight,
    class_weight,
    class_bias,
):
    devices = lax.axis_size("head")
    me = lax.axis_index("head")
    showers, local, width = queries.shape
    length = local * devices
    group = devices // showers
    team = devices // TEAMS
    outer = TEAMS
    features = width // group
    slabs = features // LANES
    each = local // POOL
    windows = length // POOL
    classes = class_weight.shape[1]
    placed = me // team
    rows = outer * each
    block = showers * each
    total = showers * rows

    def swap(x, bit):
        return lax.ppermute(x, "head", [(d, d ^ bit) for d in range(devices)])

    chunks = [(0, slabs - 1), (slabs - 1, 1)] if slabs > 1 else [(0, 1)]

    valid = (slot_positions < counts[:, None]).astype(jnp.float32)
    here = jnp.sum(valid.reshape(block, POOL), axis=1, keepdims=True)
    here = jnp.broadcast_to(here, (block, LANES))

    tokens = (slot_positions, counts, queries, keys, values)
    sent = pack(*tokens, *chunks[0], devices)

    def exchange(x):
        got = lax.all_to_all(x, "head", 0, 0, tiled=True)
        return got.reshape(length, x.shape[2])

    received = [exchange(sent)]

    order = np.arange(windows).reshape(outer, team, each).transpose(1, 0, 2).reshape(windows)
    pool = jnp.asarray(order, jnp.int32)[:, None] == jnp.arange(length, dtype=jnp.int32)[None] // POOL
    pool = pool.astype(jnp.bfloat16)

    shower_counts = counts.astype(jnp.float32)
    row_counts = jnp.tile(jnp.repeat(shower_counts, each), outer)
    row_counts = jnp.broadcast_to(row_counts[:, None], (total, LANES))
    source = np.arange(total).reshape(showers, outer, each).transpose(1, 0, 2).reshape(total)
    perm = jnp.asarray(source, jnp.int32)[:, None] == jnp.arange(total, dtype=jnp.int32)[None]
    perm = perm.astype(jnp.bfloat16)
    embedding = sinusoid(timesteps, time_weight.shape[0]).astype(jnp.bfloat16)
    modulation = jnp.dot(embedding, time_weight, preferred_element_type=jnp.float32)
    shifts = jnp.repeat(modulation[:, :width], each, axis=0)
    scales = jnp.repeat(1.0 + modulation[:, width:], each, axis=0)
    gain = norm_gain.reshape(1, width)

    target = (labels[:, None] == jnp.arange(classes, dtype=jnp.int32)[None]).astype(jnp.float32)
    spread = jnp.asarray(
        np.repeat(np.eye(showers), each, axis=0).astype(np.float32)
    )
    spread_counts = jnp.broadcast_to(shower_counts[:, None], (showers, classes))
    heads_in = (spread_counts, class_bias.reshape(1, classes), target, spread)
    fixed = (perm, gain, scales, shifts)
    late = (row_counts, class_weight)
    def gather(x):
        found = {0: x}
        bit = team // 2
        while bit:
            found.update({m ^ bit: swap(piece, bit) for m, piece in found.items()})
            bit //= 2
        return [found[m] for m in range(team)]

    class_map = jnp.dot(down_weight, class_weight, preferred_element_type=jnp.float32)
    up_weight, class_map, fixed, late, heads_in, pool = lax.optimization_barrier(
        (up_weight, class_map, fixed, late, heads_in, pool)
    )
    class_map = gather(class_map)
    gates = gather(gate_weight)
    ups = gather(up_weight)
    sent, gates, ups, class_map = lax.optimization_barrier(
        ([pack(*tokens, *chunk, devices) for chunk in chunks[1:]], gates, ups, class_map)
    )
    received += [exchange(x) for x in sent]

    attention = None
    pooled = []
    for qkv, (first, count) in zip(received, chunks):
        head = HEAD if first + count == slabs else 0
        attention, part = attend(
            qkv, pool, first, count, 2 * slabs, devices, rows, head, attention
        )
        if pooled:
            part, pooled[-1] = lax.optimization_barrier((part, pooled[-1]))
        pooled.append(lax.all_to_all(part, "head", 0, 0, tiled=True))

    units = gate_weight.shape[1]

    inside = pl.BlockSpec(memory_space=pltpu.VMEM)
    outside = pl.BlockSpec(memory_space=pl.ANY)
    side = jax.ShapeDtypeStruct((team, total, units), jnp.float32)
    members = [x for member in zip(gates, ups, class_map) for x in member]
    operands = [*pooled, *fixed, *late, *members]

    def buffers(xs):
        return [pltpu.VMEM(x.shape, x.dtype) for x in xs]

    partial, gate_side, up_side, own_x = pl.pallas_call(
        functools.partial(forward_kernel, [count * LANES for _, count in chunks], team, rows),
        out_shape=(
            jax.ShapeDtypeStruct((devices, showers, classes), jnp.float32),
            side,
            side,
            jax.ShapeDtypeStruct((block, width), jnp.float32),
        ),
        in_specs=[pl.BlockSpec(memory_space=pltpu.SMEM)] + [outside] * len(operands),
        out_specs=(inside, outside, outside, inside),
        scratch_shapes=buffers(operands)
        + [
            pltpu.VMEM((total, width), jnp.float32),
            pltpu.VMEM((total, width), jnp.bfloat16),
            pltpu.VMEM((LANES, LANES), jnp.float32),
            pltpu.VMEM(side.shape, side.dtype),
            pltpu.VMEM(side.shape, side.dtype),
            pltpu.SemaphoreType.DMA((len(operands),)),
            pltpu.SemaphoreType.DMA((2 * team,)),
        ],
        compiler_params=pltpu.CompilerParams(vmem_limit_bytes=58 * MIB),
        name="classifier_forward",
    )(jnp.stack([placed, me % team]).astype(jnp.int32), *operands)

    parts = lax.all_to_all(partial, "head", 0, 0, tiled=True)
    grads, miss = pl.pallas_call(
        functools.partial(backward_kernel, team),
        out_shape=(
            jax.ShapeDtypeStruct((outer, block, width), jnp.bfloat16),
            jax.ShapeDtypeStruct((showers, classes), jnp.float32),
        ),
        in_specs=[inside] * (1 + len(heads_in)) + [outside] * (len(members) + 2),
        scratch_shapes=buffers(members)
        + [
            pltpu.VMEM(side.shape, side.dtype),
            pltpu.VMEM(side.shape, side.dtype),
            pltpu.VMEM((total, width), jnp.float32),
            pltpu.SemaphoreType.DMA((5 * team,)),
        ],
        compiler_params=pltpu.CompilerParams(vmem_limit_bytes=58 * MIB),
        name="classifier_backward",
    )(parts, *heads_in, *members, gate_side, up_side)

    lines = [[o * team + m for o in range(outer)] for m in range(team)]
    grads = lax.all_to_all(grads, "head", 0, 0, axis_index_groups=lines, tiled=True)
    feature_grad = mm(miss, class_weight.astype(jnp.float32), NT, HIGH)
    here = here.reshape(showers, each, LANES)[:, :, :1] / shower_counts[:, None, None]
    own_row_grads = (here * feature_grad[:, None, :]).reshape(block, width)
    guidance = pl.pallas_call(
        functools.partial(final_kernel, float(windows)),
        out_shape=jax.ShapeDtypeStruct((showers, each, width), jnp.float32),
        compiler_params=pltpu.CompilerParams(vmem_limit_bytes=58 * MIB),
        name="norm_backward",
    )(grads, own_x, gain, scales, own_row_grads)
    return (attention.transpose(0, 2, 1), guidance)


def solution(mesh):
    in_specs = (
        P("parts", "head", None),
        P("parts", "head", None),
        P("parts", "head", None),
        P("parts", "head"),
        P("parts"),
        P("parts"),
        P("parts"),
        P(),
        P(),
        P(None, "head"),
        P(None, "head"),
        P("head", None),
        P(),
        P(),
    )
    out_specs = (P(("parts", "head"), None, None), P("parts", "head", None))
    return jax.shard_map(body, mesh=mesh, in_specs=in_specs, out_specs=out_specs, check_vma=False)
```

```python
import functools
import math

import jax
import jax.numpy as jnp
import numpy as np
from jax import lax
from jax.experimental import pallas as pl
from jax.experimental.pallas import tpu as pltpu
from jax.sharding import PartitionSpec as P

HEADS = 32
POOL = 16
LANES = 128
MASKED = -1e30
HEAD = 16
TEAMS = 8
ABSENT = 64.0
epsilon = 1e-06
HIGH = lax.Precision.HIGHEST
NT = (((1,), (1,)), ((), ()))
TN = (((0,), (0,)), ((), ()))
NN = (((1,), (0,)), ((), ()))
MIB = 1 << 20


def mm(a, b, dims=NN, precision=None):
    return lax.dot_general(a, b, dims, precision=precision, preferred_element_type=jnp.float32)


def sinusoid(steps, embed_width):
    half_width = embed_width // 2
    frequency = jnp.exp(-math.log(10000.0) * jnp.arange(half_width, dtype=jnp.float32) / half_width)
    angles = steps.astype(jnp.float32)[:, None] * frequency[None, :]
    return jnp.concatenate([jnp.cos(angles), jnp.sin(angles)], axis=1)


def pack_kernel(first, count, slot_ref, count_ref, q_ref, k_ref, v_ref, out_ref, packed, sems, out_sems):
    showers, group, local, _ = packed.shape
    features = q_ref.shape[2] // group
    size = count * LANES
    arriving = []
    for m in range(group):
        at = m * features + first * LANES
        for t, ref in enumerate((q_ref, k_ref, v_ref)):
            place = packed.at[:, m, :, t * size : (t + 1) * size]
            copy = pltpu.make_async_copy(ref.at[:, :, at : at + size], place, sems.at[3 * m + t])
            copy.start()
            arriving.append(copy)
    square = (local, local)
    diagonal = lax.broadcasted_iota(jnp.int32, square, 0) == lax.broadcasted_iota(
        jnp.int32, square, 1
    )
    columns = []
    for s in range(showers):
        valid = (slot_ref[s : s + 1, :] < count_ref[s]).astype(jnp.float32)
        columns.append(jnp.sum(jnp.where(diagonal, valid, 0.0), axis=1, keepdims=True) > 0.5)
    leaving = []
    for m in range(group):
        for copy in arriving[3 * m : 3 * m + 3]:
            copy.wait()
        for s in range(showers):
            part = packed[s, m, :, size : 2 * size]
            packed[s, m, :, size : 2 * size] = jnp.where(
                columns[s], part, jnp.asarray(ABSENT, part.dtype)
            )
        copy = pltpu.make_async_copy(packed.at[:, m], out_ref.at[:, m], out_sems.at[m])
        copy.start()
        leaving.append(copy)
    for copy in leaving:
        copy.wait()


def pack(slot_positions, counts, queries, keys, values, first, count, devices):
    showers, local, width = queries.shape
    group = devices // showers
    shape = (showers, group, local, 3 * count * LANES)
    outside = pl.BlockSpec(memory_space=pl.ANY)
    packed = pl.pallas_call(
        functools.partial(pack_kernel, first, count),
        out_shape=jax.ShapeDtypeStruct(shape, jnp.bfloat16),
        in_specs=[
            pl.BlockSpec(memory_space=pltpu.VMEM),
            pl.BlockSpec(memory_space=pltpu.SMEM),
            outside,
            outside,
            outside,
        ],
        out_specs=outside,
        scratch_shapes=[
            pltpu.VMEM(shape, jnp.bfloat16),
            pltpu.SemaphoreType.DMA((3 * group,)),
            pltpu.SemaphoreType.DMA((group,)),
        ],
        compiler_params=pltpu.CompilerParams(vmem_limit_bytes=58 * MIB),
        name="pack",
    )(slot_positions, counts, queries, keys, values)
    return packed.reshape((devices,) + shape[2:])


def attend_kernel(block, head, q_ref, k_ref, v_ref, pool_ref, *rest):
    att_ref, pooled_ref = rest[-2:]
    length = q_ref.shape[0]
    half = LANES // 2
    lane = lax.broadcasted_iota(jnp.int32, (1, LANES), 1)
    low = lane < half
    keys = k_ref[...]
    rows = v_ref[...]
    one = jnp.ones_like(rows)
    present = jnp.where(keys.astype(jnp.float32) < 0.5 * ABSENT, 1.0, 0.0).astype(jnp.bfloat16)
    pick = jnp.broadcast_to(jnp.where(lane == 0, 1.0, 0.0).astype(jnp.bfloat16), (8, LANES))
    valid = mm(pick, present, NT)[:1]
    bias = jnp.where(valid > 0.5, 0.0, MASKED)
    values = (jnp.where(low, rows, one), jnp.where(low, one, rows))

    for i in range(length // block):
        at = slice(i * block, (i + 1) * block)
        query = q_ref[at, :] * jnp.asarray(0.125, jnp.bfloat16)
        zero = jnp.zeros_like(query)
        outs = []
        for h in range(2):
            own = jnp.where(low, query, zero) if h == 0 else jnp.where(low, zero, query)
            scores = mm(own, keys, NT) + bias
            peak = jnp.max(scores, axis=1, keepdims=True)
            weights = jnp.exp(scores - peak).astype(jnp.bfloat16)
            outs.append(mm(weights, values[h]))
        top = jnp.where(low, outs[0], outs[1])
        total = jnp.where(low, pltpu.roll(outs[0], half, 1), pltpu.roll(outs[1], half, 1))
        mixed = ((top / total).T * valid[:, at]).astype(jnp.bfloat16)
        att_ref[0, :, at] = mixed[:half]
        att_ref[1, :, at] = mixed[half:]
    both = jnp.concatenate([att_ref[0], att_ref[1]], axis=0)
    cnt = mm(pool_ref[...], jnp.broadcast_to(valid, (LANES, length)).astype(jnp.bfloat16), NT)
    pooled = (mm(pool_ref[...], both, NT) / jnp.maximum(cnt, 1.0)).astype(jnp.bfloat16)
    rows = pooled_ref.shape[1] - head
    team = pooled.shape[0] // rows
    if head:
        ones = jnp.broadcast_to(valid, (head, length)).astype(jnp.bfloat16)
        counted = mm(ones, pool_ref[...], NT).astype(jnp.bfloat16)
    for d in range(pooled_ref.shape[0]):
        m = d % team
        pooled_ref[d, head:] = pooled[m * rows : (m + 1) * rows]
        if head:
            pooled_ref[d, :head] = counted


def attend(qkv, pool, first, count, pairs, devices, rows, head, before):
    length = qkv.shape[0]
    windows = pool.shape[0]
    head_dim = LANES // 2

    def part(which):
        return pl.BlockSpec((length, LANES), lambda j: (0, which * count + j))

    def whole(shape):
        return pl.BlockSpec(shape, lambda j: (0, 0))

    in_specs = [
        part(0),
        part(1),
        part(2),
        whole((windows, length)),
    ]
    operands = [qkv, qkv, qkv, pool]
    aliases = {}
    if before is not None:
        in_specs.append(pl.BlockSpec(memory_space=pl.ANY))
        operands.append(before)
        aliases = {4: 0}
    return pl.pallas_call(
        functools.partial(attend_kernel, min(512, length), head),
        grid=(count,),
        out_shape=(
            jax.ShapeDtypeStruct((pairs, head_dim, length), jnp.bfloat16),
            jax.ShapeDtypeStruct((devices, head + rows, count * LANES), jnp.bfloat16),
        ),
        in_specs=in_specs,
        out_specs=(
            pl.BlockSpec((2, head_dim, length), lambda j: (first + j, 0, 0)),
            pl.BlockSpec((devices, head + rows, LANES), lambda j: (0, 0, j)),
        ),
        input_output_aliases=aliases,
        compiler_params=pltpu.CompilerParams(vmem_limit_bytes=40 * MIB),
        cost_estimate=pl.CostEstimate(
            flops=count * 2 * 4 * length * length * head_dim,
            bytes_accessed=count * length * LANES * 8,
            transcendentals=count * 2 * length * length,
        ),
        name="attend",
    )(*operands)


def forward_kernel(lanes, team, rows, place_ref, *refs):
    n = len(lanes)
    inputs = n + 6 + 3 * team
    sources, (copies_ref, ga_out, aa_out, own_x_ref) = refs[:inputs], refs[inputs : inputs + 4]
    buffers = refs[inputs + 4 : 2 * inputs + 4]
    gathered, normed, counted, ga_ref, aa_ref, sems, out_sems = refs[2 * inputs + 4 :]
    arriving = [
        pltpu.make_async_copy(source, buffer, sems.at[i])
        for i, (source, buffer) in enumerate(zip(sources, buffers))
    ]
    first = n + 6
    for copy in arriving[: first + 3]:
        copy.start()

    def get(i):
        arriving[i].wait()
        return buffers[i]

    def start_member(i):
        if i < team:
            for copy in arriving[first + 3 * i : first + 3 * i + 3]:
                copy.start()

    showers = copies_ref.shape[1]
    group = buffers[0].shape[0] // showers
    width = gathered.shape[1]
    block = own_x_ref.shape[0]
    total = rows * showers
    x_refs = [get(i) for i in range(n)]
    start_member(1)
    for s in range(showers):
        for m in range(group):
            at = m * (width // group)
            for ref, size in zip(x_refs, lanes):
                part = ref[s * group + m, ref.shape[1] - rows :]
                gathered[s * rows : (s + 1) * rows, at : at + size] = part.astype(jnp.float32)
                at += size
    packed = gathered[...].astype(jnp.bfloat16)
    perm_ref, gain_ref, scale_ref, shift_ref = [get(n + i) for i in range(4)]
    gathered[...] = mm(perm_ref[...], packed)
    for b in range(total // block):
        at = slice(b * block, (b + 1) * block)
        x = gathered[at]
        inverse = lax.rsqrt(jnp.mean(x * x, axis=1, keepdims=True) + epsilon)
        normed[at] = (x * inverse * gain_ref[...] * scale_ref[...] + shift_ref[...]).astype(
            jnp.bfloat16
        )
    own_x_ref[...] = gathered[pl.ds(pl.multiple_of(place_ref[0] * block, block), block), :]
    counts_ref, class_ref = [get(n + 4 + i) for i in range(2)]
    counted[...] = jnp.zeros(counted.shape, jnp.float32)
    for s in range(showers):
        counted[s : s + 1] = x_refs[-1][s * group, :HEAD].astype(jnp.float32)[:1]
    shape = (total, LANES)
    row = lax.broadcasted_iota(jnp.int32, shape, 0)
    lane = lax.broadcasted_iota(jnp.int32, shape, 1)
    each = block // showers
    from_lane = place_ref[1] * rows + row // block * each + row % each
    pick = jnp.where(lane == from_lane, 1.0, 0.0).astype(jnp.bfloat16)
    cnt_of = mm(pick, counted[...].astype(jnp.bfloat16), NT)
    cnt_of = jnp.where(lane == row % block // each, cnt_of, 0.0)
    cnt = jnp.sum(cnt_of, axis=1, keepdims=True)
    own_cnt_of = jnp.where(row // block == place_ref[0], cnt_of, 0.0).astype(jnp.bfloat16)
    cnt_of = cnt_of.astype(jnp.bfloat16)
    sums = mm(own_cnt_of, gathered[...].astype(jnp.bfloat16), TN)[:showers]
    logits = mm(sums, class_ref[...].astype(jnp.float32), precision=HIGH)
    coef = cnt / counts_ref[...][:, :1]
    leaving = []
    for i in range(team):
        gate_ref, up_ref, map_ref = [get(first + 3 * i + j) for j in range(3)]
        start_member(i + 2)
        gate = mm(normed[...], gate_ref[...])
        up = mm(normed[...], up_ref[...])
        sigma = jax.nn.sigmoid(gate)
        activated = gate * sigma
        hidden = (activated * up).astype(jnp.bfloat16)
        logits = logits + mm(mm(cnt_of, hidden, TN)[:showers], map_ref[...], precision=HIGH)
        ga_ref[i] = (coef * (up * sigma * (1.0 + gate * (1.0 - sigma)))).astype(jnp.bfloat16)
        aa_ref[i] = (coef * activated).astype(jnp.bfloat16)
        for j, (kept, out) in enumerate(((ga_ref, ga_out), (aa_ref, aa_out))):
            copy = pltpu.make_async_copy(kept.at[i], out.at[i], out_sems.at[2 * i + j])
            copy.start()
            leaving.append(copy)
    for d in range(copies_ref.shape[0]):
        copies_ref[d] = logits
    for copy in leaving:
        copy.wait()


def backward_kernel(team, parts_ref, counts_ref, bias_ref, target_ref, spread_ref, *refs):
    sources = refs[: 3 * team]
    ga_in, aa_in, dn_ref, miss_ref = refs[3 * team : 3 * team + 4]
    buffers = refs[3 * team + 4 : 6 * team + 4]
    ga_ref, aa_ref, total, sems = refs[6 * team + 4 :]
    arriving = []
    for i in range(team):
        pairs = [(sources[3 * i + 2], buffers[3 * i + 2]), (ga_in.at[i], ga_ref.at[i])]
        pairs += [(aa_in.at[i], aa_ref.at[i])]
        pairs += [(sources[3 * i + j], buffers[3 * i + j]) for j in range(2)]
        arriving.append(
            [
                pltpu.make_async_copy(source, buffer, sems.at[5 * i + j])
                for j, (source, buffer) in enumerate(pairs)
            ]
        )

    def start_member(i):
        if i < team:
            for copy in arriving[i]:
                copy.start()

    start_member(0)
    start_member(1)
    blocks, block, _ = dn_ref.shape
    logits = jnp.sum(parts_ref[...], axis=0) / counts_ref[...] + bias_ref[...]
    exponent = jnp.exp(logits - jnp.max(logits, axis=1, keepdims=True))
    miss = target_ref[...] - exponent / jnp.sum(exponent, axis=1, keepdims=True)
    miss_ref[...] = miss
    spread = mm(spread_ref[...], miss, precision=HIGH)
    for i in range(team):
        gate_ref, up_ref, map_ref = buffers[3 * i : 3 * i + 3]
        for copy in arriving[i]:
            copy.wait()
        start_member(i + 2)
        wide = mm(spread, map_ref[...], NT, HIGH)
        wide = jnp.concatenate([wide] * blocks, axis=0)
        gate_grad = (wide * ga_ref[i].astype(jnp.float32)).astype(jnp.bfloat16)
        up_grad = (wide * aa_ref[i].astype(jnp.float32)).astype(jnp.bfloat16)
        term = mm(gate_grad, gate_ref[...], NT) + mm(up_grad, up_ref[...], NT)
        if i == 0:
            total[...] = term
        elif i < team - 1:
            total[...] += term
        else:
            term = (total[...] + term).astype(jnp.bfloat16)
            for b in range(blocks):
                dn_ref[b] = term[b * block : (b + 1) * block]


def final_kernel(windows, dn_ref, x_ref, gain_ref, scale_ref, dy_ref, out_ref):
    total = dn_ref[0].astype(jnp.float32)
    for b in range(1, dn_ref.shape[0]):
        total = total + dn_ref[b].astype(jnp.float32)
    x = x_ref[...]
    inverse = lax.rsqrt(jnp.mean(x * x, axis=1, keepdims=True) + epsilon)
    unit = x * inverse
    grad = total * gain_ref[...] * scale_ref[...]
    back = inverse * (grad - unit * jnp.mean(grad * unit, axis=1, keepdims=True))
    value = windows * (dy_ref[...] + back)
    each = out_ref.shape[1]
    for s in range(out_ref.shape[0]):
        out_ref[s] = value[s * each : (s + 1) * each]


def body(
    queries,
    keys,
    values,
    slot_positions,
    counts,
    timesteps,
    labels,
    time_weight,
    norm_gain,
    gate_weight,
    up_weight,
    down_weight,
    class_weight,
    class_bias,
):
    devices = lax.axis_size("head")
    me = lax.axis_index("head")
    showers, local, width = queries.shape
    length = local * devices
    group = devices // showers
    team = devices // TEAMS
    outer = TEAMS
    features = width // group
    slabs = features // LANES
    each = local // POOL
    windows = length // POOL
    classes = class_weight.shape[1]
    placed = me // team
    rows = outer * each
    block = showers * each
    total = showers * rows

    def swap(x, bit):
        return lax.ppermute(x, "head", [(d, d ^ bit) for d in range(devices)])

    chunks = [(0, slabs - 1), (slabs - 1, 1)] if slabs > 1 else [(0, 1)]

    valid = (slot_positions < counts[:, None]).astype(jnp.float32)
    here = jnp.sum(valid.reshape(block, POOL), axis=1, keepdims=True)
    here = jnp.broadcast_to(here, (block, LANES))

    tokens = (slot_positions, counts, queries, keys, values)
    sent = pack(*tokens, *chunks[0], devices)

    def exchange(x):
        got = lax.all_to_all(x, "head", 0, 0, tiled=True)
        return got.reshape(length, x.shape[2])

    received = [exchange(sent)]

    order = np.arange(windows).reshape(outer, team, each).transpose(1, 0, 2).reshape(windows)
    pool = jnp.asarray(order, jnp.int32)[:, None] == jnp.arange(length, dtype=jnp.int32)[None] // POOL
    pool = pool.astype(jnp.bfloat16)

    shower_counts = counts.astype(jnp.float32)
    row_counts = jnp.tile(jnp.repeat(shower_counts, each), outer)
    row_counts = jnp.broadcast_to(row_counts[:, None], (total, LANES))
    source = np.arange(total).reshape(showers, outer, each).transpose(1, 0, 2).reshape(total)
    perm = jnp.asarray(source, jnp.int32)[:, None] == jnp.arange(total, dtype=jnp.int32)[None]
    perm = perm.astype(jnp.bfloat16)
    embedding = sinusoid(timesteps, time_weight.shape[0]).astype(jnp.bfloat16)
    modulation = jnp.dot(embedding, time_weight, preferred_element_type=jnp.float32)
    shifts = jnp.repeat(modulation[:, :width], each, axis=0)
    scales = jnp.repeat(1.0 + modulation[:, width:], each, axis=0)
    gain = norm_gain.reshape(1, width)

    target = (labels[:, None] == jnp.arange(classes, dtype=jnp.int32)[None]).astype(jnp.float32)
    spread = jnp.asarray(
        np.repeat(np.eye(showers), each, axis=0).astype(np.float32)
    )
    spread_counts = jnp.broadcast_to(shower_counts[:, None], (showers, classes))
    heads_in = (spread_counts, class_bias.reshape(1, classes), target, spread)
    fixed = (perm, gain, scales, shifts)
    late = (row_counts, class_weight)
    def gather(x):
        found = {0: x}
        bit = team // 2
        while bit:
            found.update({m ^ bit: swap(piece, bit) for m, piece in found.items()})
            bit //= 2
        return [found[m] for m in range(team)]

    class_map = jnp.dot(down_weight, class_weight, preferred_element_type=jnp.float32)
    sent = [pack(*tokens, *chunk, devices) for chunk in chunks[1:]]
    sent, up_weight, class_map, fixed, late, heads_in, pool = lax.optimization_barrier(
        (sent, up_weight, class_map, fixed, late, heads_in, pool)
    )
    class_map = gather(class_map)
    gates = gather(gate_weight)
    ups = gather(up_weight)
    sent, gates, ups, class_map = lax.optimization_barrier(
        (sent, gates, ups, class_map)
    )
    received += [exchange(x) for x in sent]

    attention = None
    pooled = []
    for qkv, (first, count) in zip(received, chunks):
        head = HEAD if first + count == slabs else 0
        attention, part = attend(
            qkv, pool, first, count, 2 * slabs, devices, rows, head, attention
        )
        if pooled:
            part, pooled[-1] = lax.optimization_barrier((part, pooled[-1]))
        pooled.append(lax.all_to_all(part, "head", 0, 0, tiled=True))

    units = gate_weight.shape[1]

    inside = pl.BlockSpec(memory_space=pltpu.VMEM)
    outside = pl.BlockSpec(memory_space=pl.ANY)
    side = jax.ShapeDtypeStruct((team, total, units), jnp.bfloat16)
    members = [x for member in zip(gates, ups, class_map) for x in member]
    operands = [*pooled, *fixed, *late, *members]

    def buffers(xs):
        return [pltpu.VMEM(x.shape, x.dtype) for x in xs]

    partial, gate_side, up_side, own_x = pl.pallas_call(
        functools.partial(forward_kernel, [count * LANES for _, count in chunks], team, rows),
        out_shape=(
            jax.ShapeDtypeStruct((devices, showers, classes), jnp.float32),
            side,
            side,
            jax.ShapeDtypeStruct((block, width), jnp.float32),
        ),
        in_specs=[pl.BlockSpec(memory_space=pltpu.SMEM)] + [outside] * len(operands),
        out_specs=(inside, outside, outside, inside),
        scratch_shapes=buffers(operands)
        + [
            pltpu.VMEM((total, width), jnp.float32),
            pltpu.VMEM((total, width), jnp.bfloat16),
            pltpu.VMEM((LANES, LANES), jnp.float32),
            pltpu.VMEM(side.shape, side.dtype),
            pltpu.VMEM(side.shape, side.dtype),
            pltpu.SemaphoreType.DMA((len(operands),)),
            pltpu.SemaphoreType.DMA((2 * team,)),
        ],
        compiler_params=pltpu.CompilerParams(vmem_limit_bytes=58 * MIB),
        name="classifier_forward",
    )(jnp.stack([placed, me % team]).astype(jnp.int32), *operands)

    parts = lax.all_to_all(partial, "head", 0, 0, tiled=True)
    grads, miss = pl.pallas_call(
        functools.partial(backward_kernel, team),
        out_shape=(
            jax.ShapeDtypeStruct((outer, block, width), jnp.bfloat16),
            jax.ShapeDtypeStruct((showers, classes), jnp.float32),
        ),
        in_specs=[inside] * (1 + len(heads_in)) + [outside] * (len(members) + 2),
        scratch_shapes=buffers(members)
        + [
            pltpu.VMEM(side.shape, side.dtype),
            pltpu.VMEM(side.shape, side.dtype),
            pltpu.VMEM((total, width), jnp.float32),
            pltpu.SemaphoreType.DMA((5 * team,)),
        ],
        compiler_params=pltpu.CompilerParams(vmem_limit_bytes=58 * MIB),
        name="classifier_backward",
    )(parts, *heads_in, *members, gate_side, up_side)

    lines = [[o * team + m for o in range(outer)] for m in range(team)]
    grads = lax.all_to_all(grads, "head", 0, 0, axis_index_groups=lines, tiled=True)
    feature_grad = mm(miss, class_weight.astype(jnp.float32), NT, HIGH)
    here = here.reshape(showers, each, LANES)[:, :, :1] / shower_counts[:, None, None]
    own_row_grads = (here * feature_grad[:, None, :]).reshape(block, width)
    guidance = pl.pallas_call(
        functools.partial(final_kernel, float(windows)),
        out_shape=jax.ShapeDtypeStruct((showers, each, width), jnp.float32),
        compiler_params=pltpu.CompilerParams(vmem_limit_bytes=58 * MIB),
        name="norm_backward",
    )(grads, own_x, gain, scales, own_row_grads)
    return (attention.transpose(0, 2, 1), guidance)


def solution(mesh):
    in_specs = (
        P("parts", "head", None),
        P("parts", "head", None),
        P("parts", "head", None),
        P("parts", "head"),
        P("parts"),
        P("parts"),
        P("parts"),
        P(),
        P(),
        P(None, "head"),
        P(None, "head"),
        P("head", None),
        P(),
        P(),
    )
    out_specs = (P(("parts", "head"), None, None), P("parts", "head", None))
    return jax.shard_map(body, mesh=mesh, in_specs=in_specs, out_specs=out_specs, check_vma=False)
```

```python
import functools
import math

import jax
import jax.numpy as jnp
import numpy as np
from jax import lax
from jax.experimental import pallas as pl
from jax.experimental.pallas import tpu as pltpu
from jax.sharding import PartitionSpec as P

HEADS = 32
POOL = 16
LANES = 128
MASKED = -1e30
HEAD = 16
TEAM = 8
ABSENT = 64.0
epsilon = 1e-06
HIGH = lax.Precision.HIGHEST
NT = (((1,), (1,)), ((), ()))
TN = (((0,), (0,)), ((), ()))
NN = (((1,), (0,)), ((), ()))
MIB = 1 << 20


def mm(a, b, dims=NN, precision=None):
    return lax.dot_general(a, b, dims, precision=precision, preferred_element_type=jnp.float32)


def sinusoid(steps, embed_width):
    half_width = embed_width // 2
    frequency = jnp.exp(-math.log(10000.0) * jnp.arange(half_width, dtype=jnp.float32) / half_width)
    angles = steps.astype(jnp.float32)[:, None] * frequency[None, :]
    return jnp.concatenate([jnp.cos(angles), jnp.sin(angles)], axis=1)


def pack_kernel(first, count, slot_ref, count_ref, q_ref, k_ref, v_ref, out_ref, packed, sems, out_sems):
    showers, group, local, _ = packed.shape
    features = q_ref.shape[2] // group
    size = count * LANES
    arriving = []
    for m in range(group):
        at = m * features + first * LANES
        for t, ref in enumerate((q_ref, k_ref, v_ref)):
            place = packed.at[:, m, :, t * size : (t + 1) * size]
            copy = pltpu.make_async_copy(ref.at[:, :, at : at + size], place, sems.at[3 * m + t])
            copy.start()
            arriving.append(copy)
    square = (local, local)
    diagonal = lax.broadcasted_iota(jnp.int32, square, 0) == lax.broadcasted_iota(
        jnp.int32, square, 1
    )
    columns = []
    for s in range(showers):
        valid = (slot_ref[s : s + 1, :] < count_ref[s]).astype(jnp.float32)
        columns.append(jnp.sum(jnp.where(diagonal, valid, 0.0), axis=1, keepdims=True) > 0.5)
    leaving = []
    for m in range(group):
        for copy in arriving[3 * m : 3 * m + 3]:
            copy.wait()
        for s in range(showers):
            part = packed[s, m, :, size : 2 * size]
            packed[s, m, :, size : 2 * size] = jnp.where(
                columns[s], part, jnp.asarray(ABSENT, part.dtype)
            )
        copy = pltpu.make_async_copy(packed.at[:, m], out_ref.at[:, m], out_sems.at[m])
        copy.start()
        leaving.append(copy)
    for copy in leaving:
        copy.wait()


def pack(slot_positions, counts, queries, keys, values, first, count, devices):
    showers, local, width = queries.shape
    group = devices // showers
    shape = (showers, group, local, 3 * count * LANES)
    outside = pl.BlockSpec(memory_space=pl.ANY)
    packed = pl.pallas_call(
        functools.partial(pack_kernel, first, count),
        out_shape=jax.ShapeDtypeStruct(shape, jnp.bfloat16),
        in_specs=[
            pl.BlockSpec(memory_space=pltpu.VMEM),
            pl.BlockSpec(memory_space=pltpu.SMEM),
            outside,
            outside,
            outside,
        ],
        out_specs=outside,
        scratch_shapes=[
            pltpu.VMEM(shape, jnp.bfloat16),
            pltpu.SemaphoreType.DMA((3 * group,)),
            pltpu.SemaphoreType.DMA((group,)),
        ],
        compiler_params=pltpu.CompilerParams(vmem_limit_bytes=58 * MIB),
        name="pack",
    )(slot_positions, counts, queries, keys, values)
    return packed.reshape((devices,) + shape[2:])


def attend_kernel(block, head, q_ref, k_ref, v_ref, pool_ref, *rest):
    att_ref, pooled_ref = rest[-2:]
    length = q_ref.shape[0]
    half = LANES // 2
    lane = lax.broadcasted_iota(jnp.int32, (1, LANES), 1)
    low = lane < half
    keys = k_ref[...]
    rows = v_ref[...]
    one = jnp.ones_like(rows)
    present = jnp.where(keys.astype(jnp.float32) < 0.5 * ABSENT, 1.0, 0.0).astype(jnp.bfloat16)
    pick = jnp.broadcast_to(jnp.where(lane == 0, 1.0, 0.0).astype(jnp.bfloat16), (8, LANES))
    valid = mm(pick, present, NT)[:1]
    bias = jnp.where(valid > 0.5, 0.0, MASKED)
    values = (jnp.where(low, rows, one), jnp.where(low, one, rows))

    for i in range(length // block):
        at = slice(i * block, (i + 1) * block)
        query = q_ref[at, :] * jnp.asarray(0.125, jnp.bfloat16)
        zero = jnp.zeros_like(query)
        outs = []
        for h in range(2):
            own = jnp.where(low, query, zero) if h == 0 else jnp.where(low, zero, query)
            scores = mm(own, keys, NT) + bias
            peak = jnp.max(scores, axis=1, keepdims=True)
            weights = jnp.exp(scores - peak).astype(jnp.bfloat16)
            outs.append(mm(weights, values[h]))
        top = jnp.where(low, outs[0], outs[1])
        total = jnp.where(low, pltpu.roll(outs[0], half, 1), pltpu.roll(outs[1], half, 1))
        mixed = ((top / total).T * valid[:, at]).astype(jnp.bfloat16)
        att_ref[0, :, at] = mixed[:half]
        att_ref[1, :, at] = mixed[half:]
    both = jnp.concatenate([att_ref[0], att_ref[1]], axis=0)
    cnt = mm(pool_ref[...], jnp.broadcast_to(valid, (LANES, length)).astype(jnp.bfloat16), NT)
    pooled = (mm(pool_ref[...], both, NT) / jnp.maximum(cnt, 1.0)).astype(jnp.bfloat16)
    rows = pooled_ref.shape[1] - head
    team = pooled.shape[0] // rows
    if head:
        ones = jnp.broadcast_to(valid, (head, length)).astype(jnp.bfloat16)
        counted = mm(ones, pool_ref[...], NT).astype(jnp.bfloat16)
    for d in range(pooled_ref.shape[0]):
        m = d % team
        pooled_ref[d, head:] = pooled[m * rows : (m + 1) * rows]
        if head:
            pooled_ref[d, :head] = counted


def attend(qkv, pool, first, count, pairs, devices, rows, head, before):
    length = qkv.shape[0]
    windows = pool.shape[0]
    head_dim = LANES // 2

    def part(which):
        return pl.BlockSpec((length, LANES), lambda j: (0, which * count + j))

    def whole(shape):
        return pl.BlockSpec(shape, lambda j: (0, 0))

    in_specs = [
        part(0),
        part(1),
        part(2),
        whole((windows, length)),
    ]
    operands = [qkv, qkv, qkv, pool]
    aliases = {}
    if before is not None:
        in_specs.append(pl.BlockSpec(memory_space=pl.ANY))
        operands.append(before)
        aliases = {4: 0}
    return pl.pallas_call(
        functools.partial(attend_kernel, min(512, length), head),
        grid=(count,),
        out_shape=(
            jax.ShapeDtypeStruct((pairs, head_dim, length), jnp.bfloat16),
            jax.ShapeDtypeStruct((devices, head + rows, count * LANES), jnp.bfloat16),
        ),
        in_specs=in_specs,
        out_specs=(
            pl.BlockSpec((2, head_dim, length), lambda j: (first + j, 0, 0)),
            pl.BlockSpec((devices, head + rows, LANES), lambda j: (0, 0, j)),
        ),
        input_output_aliases=aliases,
        compiler_params=pltpu.CompilerParams(vmem_limit_bytes=40 * MIB),
        cost_estimate=pl.CostEstimate(
            flops=count * 2 * 4 * length * length * head_dim,
            bytes_accessed=count * length * LANES * 8,
            transcendentals=count * 2 * length * length,
        ),
        name="attend",
    )(*operands)


def split(x):
    coarse = x.astype(jnp.bfloat16)
    return coarse, (x - coarse.astype(jnp.float32)).astype(jnp.bfloat16)


def forward_kernel(lanes, team, rows, place_ref, *refs):
    n = len(lanes)
    inputs = n + 6 + 2 * team
    sources, (copies_ref, ga_out, aa_out, own_x_ref) = refs[:inputs], refs[inputs : inputs + 4]
    buffers = refs[inputs + 4 : 2 * inputs + 4]
    gathered, normed, counted, ga_ref, aa_ref, sems, out_sems = refs[2 * inputs + 4 :]
    arriving = [
        pltpu.make_async_copy(source, buffer, sems.at[i])
        for i, (source, buffer) in enumerate(zip(sources, buffers))
    ]
    first = n + 6
    for copy in arriving[: first + 2]:
        copy.start()

    def get(i):
        arriving[i].wait()
        return buffers[i]

    def start_member(i):
        if i < team:
            for copy in arriving[first + 2 * i : first + 2 * i + 2]:
                copy.start()

    showers, classes = copies_ref.shape[1:]
    group = buffers[0].shape[0] // showers
    width = gathered.shape[1]
    block = own_x_ref.shape[0]
    total = rows * showers
    x_refs = [get(i) for i in range(n)]
    start_member(1)
    for s in range(showers):
        for m in range(group):
            at = m * (width // group)
            for ref, size in zip(x_refs, lanes):
                part = ref[s * group + m, ref.shape[1] - rows :]
                gathered[s * rows : (s + 1) * rows, at : at + size] = part.astype(jnp.float32)
                at += size
    packed = gathered[...].astype(jnp.bfloat16)
    perm_ref, gain_ref, scale_ref, shift_ref = [get(n + i) for i in range(4)]
    gathered[...] = mm(perm_ref[...], packed)
    for b in range(total // block):
        at = slice(b * block, (b + 1) * block)
        x = gathered[at]
        inverse = lax.rsqrt(jnp.mean(x * x, axis=1, keepdims=True) + epsilon)
        normed[at] = (x * inverse * gain_ref[...] * scale_ref[...] + shift_ref[...]).astype(
            jnp.bfloat16
        )
    own_x_ref[...] = gathered[pl.ds(pl.multiple_of(place_ref[0] * block, block), block), :]
    counts_ref, class_ref = [get(n + 4 + i) for i in range(2)]
    counted[...] = jnp.zeros(counted.shape, jnp.float32)
    for s in range(showers):
        counted[s : s + 1] = x_refs[-1][s * group, :HEAD].astype(jnp.float32)[:1]
    shape = (total, LANES)
    row = lax.broadcasted_iota(jnp.int32, shape, 0)
    lane = lax.broadcasted_iota(jnp.int32, shape, 1)
    each = block // showers
    from_lane = place_ref[1] * rows + row // block * each + row % each
    pick = jnp.where(lane == from_lane, 1.0, 0.0).astype(jnp.bfloat16)
    cnt_of = mm(pick, counted[...].astype(jnp.bfloat16), NT)
    cnt_of = jnp.where(lane == row % block // each, cnt_of, 0.0)
    cnt = jnp.sum(cnt_of, axis=1, keepdims=True)
    own_cnt_of = jnp.where(row // block == place_ref[0], cnt_of, 0.0).astype(jnp.bfloat16)
    cnt_of = cnt_of.astype(jnp.bfloat16)
    sums = mm(own_cnt_of, gathered[...].astype(jnp.bfloat16), TN)[:showers]
    logits = mm(sums, class_ref[...].astype(jnp.float32), precision=HIGH)
    coef = cnt / counts_ref[...][:, :1]
    leaving = []
    for i in range(team):
        gate_ref, up_ref = [get(first + 2 * i + j) for j in range(2)]
        start_member(i + 2)
        gate = mm(normed[...], gate_ref[...])
        up = mm(normed[...], up_ref[:width])
        sigma = jax.nn.sigmoid(gate)
        activated = gate * sigma
        hidden = (activated * up).astype(jnp.bfloat16)
        coarse, fine = split(mm(cnt_of, hidden, TN)[:showers])
        both = mm(coarse, up_ref[width:], NT)
        logits = logits + both[:, :classes] + both[:, classes:]
        logits = logits + mm(fine, up_ref[width : width + classes], NT)
        ga_ref[i] = (coef * (up * sigma * (1.0 + gate * (1.0 - sigma)))).astype(jnp.bfloat16)
        aa_ref[i] = (coef * activated).astype(jnp.bfloat16)
        for j, (kept, out) in enumerate(((ga_ref, ga_out), (aa_ref, aa_out))):
            copy = pltpu.make_async_copy(kept.at[i], out.at[i], out_sems.at[2 * i + j])
            copy.start()
            leaving.append(copy)
    for d in range(copies_ref.shape[0]):
        copies_ref[d] = logits
    for copy in leaving:
        copy.wait()


def backward_kernel(team, parts_ref, counts_ref, bias_ref, target_ref, spread_ref, *refs):
    sources = refs[: 2 * team]
    ga_in, aa_in, dn_ref, miss_ref = refs[2 * team : 2 * team + 4]
    buffers = refs[2 * team + 4 : 4 * team + 4]
    ga_ref, aa_ref, total, sems = refs[4 * team + 4 :]
    arriving = []
    for i in range(team):
        pairs = [(ga_in.at[i], ga_ref.at[i]), (aa_in.at[i], aa_ref.at[i])]
        pairs += [(sources[2 * i + j], buffers[2 * i + j]) for j in range(2)]
        arriving.append(
            [
                pltpu.make_async_copy(source, buffer, sems.at[4 * i + j])
                for j, (source, buffer) in enumerate(pairs)
            ]
        )

    def start_member(i):
        if i < team:
            for copy in arriving[i]:
                copy.start()

    start_member(0)
    start_member(1)
    blocks, block, _ = dn_ref.shape
    logits = jnp.sum(parts_ref[...], axis=0) / counts_ref[...] + bias_ref[...]
    exponent = jnp.exp(logits - jnp.max(logits, axis=1, keepdims=True))
    miss = target_ref[...] - exponent / jnp.sum(exponent, axis=1, keepdims=True)
    miss_ref[...] = miss
    coarse, fine = split(mm(spread_ref[...], miss, precision=HIGH))
    coarse = jnp.concatenate([coarse, coarse], axis=1)
    classes = miss.shape[1]
    width = dn_ref.shape[2]
    for i in range(team):
        gate_ref, up_ref = buffers[2 * i : 2 * i + 2]
        for copy in arriving[i]:
            copy.wait()
        start_member(i + 2)
        wide = mm(coarse, up_ref[width:]) + mm(fine, up_ref[width : width + classes])
        wide = jnp.concatenate([wide] * blocks, axis=0)
        gate_grad = (wide * ga_ref[i].astype(jnp.float32)).astype(jnp.bfloat16)
        up_grad = (wide * aa_ref[i].astype(jnp.float32)).astype(jnp.bfloat16)
        term = mm(gate_grad, gate_ref[...], NT) + mm(up_grad, up_ref[:width], NT)
        if i == 0:
            total[...] = term
        elif i < team - 1:
            total[...] += term
        else:
            term = (total[...] + term).astype(jnp.bfloat16)
            for b in range(blocks):
                dn_ref[b] = term[b * block : (b + 1) * block]


def final_kernel(windows, dn_ref, x_ref, gain_ref, scale_ref, dy_ref, out_ref):
    total = dn_ref[0].astype(jnp.float32)
    for b in range(1, dn_ref.shape[0]):
        total = total + dn_ref[b].astype(jnp.float32)
    x = x_ref[...]
    inverse = lax.rsqrt(jnp.mean(x * x, axis=1, keepdims=True) + epsilon)
    unit = x * inverse
    grad = total * gain_ref[...] * scale_ref[...]
    back = inverse * (grad - unit * jnp.mean(grad * unit, axis=1, keepdims=True))
    value = windows * (dy_ref[...] + back)
    each = out_ref.shape[1]
    for s in range(out_ref.shape[0]):
        out_ref[s] = value[s * each : (s + 1) * each]


def body(
    queries,
    keys,
    values,
    slot_positions,
    counts,
    timesteps,
    labels,
    time_weight,
    norm_gain,
    gate_weight,
    up_weight,
    down_weight,
    class_weight,
    class_bias,
):
    devices = lax.axis_size("head")
    me = lax.axis_index("head")
    showers, local, width = queries.shape
    length = local * devices
    group = devices // showers
    team = TEAM
    outer = devices // team
    features = width // group
    slabs = features // LANES
    each = local // POOL
    windows = length // POOL
    classes = class_weight.shape[1]
    placed = me // team
    rows = outer * each
    block = showers * each
    total = showers * rows

    def swap(x, bit):
        return lax.ppermute(x, "head", [(d, d ^ bit) for d in range(devices)])

    chunks = [(0, slabs - 1), (slabs - 1, 1)] if slabs > 1 else [(0, 1)]

    valid = (slot_positions < counts[:, None]).astype(jnp.float32)
    here = jnp.sum(valid.reshape(block, POOL), axis=1, keepdims=True)
    here = jnp.broadcast_to(here, (block, LANES))

    tokens = (slot_positions, counts, queries, keys, values)
    sent = pack(*tokens, *chunks[0], devices)

    def exchange(x):
        got = lax.all_to_all(x, "head", 0, 0, tiled=True)
        return got.reshape(length, x.shape[2])

    received = [exchange(sent)]

    order = np.arange(windows).reshape(outer, team, each).transpose(1, 0, 2).reshape(windows)
    pool = jnp.asarray(order, jnp.int32)[:, None] == jnp.arange(length, dtype=jnp.int32)[None] // POOL
    pool = pool.astype(jnp.bfloat16)

    shower_counts = counts.astype(jnp.float32)
    row_counts = jnp.tile(jnp.repeat(shower_counts, each), outer)
    row_counts = jnp.broadcast_to(row_counts[:, None], (total, LANES))
    source = np.arange(total).reshape(showers, outer, each).transpose(1, 0, 2).reshape(total)
    perm = jnp.asarray(source, jnp.int32)[:, None] == jnp.arange(total, dtype=jnp.int32)[None]
    perm = perm.astype(jnp.bfloat16)
    embedding = sinusoid(timesteps, time_weight.shape[0]).astype(jnp.bfloat16)
    modulation = jnp.dot(embedding, time_weight, preferred_element_type=jnp.float32)
    shifts = jnp.repeat(modulation[:, :width], each, axis=0)
    scales = jnp.repeat(1.0 + modulation[:, width:], each, axis=0)
    gain = norm_gain.reshape(1, width)

    target = (labels[:, None] == jnp.arange(classes, dtype=jnp.int32)[None]).astype(jnp.float32)
    spread = jnp.asarray(
        np.repeat(np.eye(showers), each, axis=0).astype(np.float32)
    )
    spread_counts = jnp.broadcast_to(shower_counts[:, None], (showers, classes))
    heads_in = (spread_counts, class_bias.reshape(1, classes), target, spread)
    fixed = (perm, gain, scales, shifts)
    late = (row_counts, class_weight)
    def spread_out(x, bits):
        found = {0: x}
        for bit in bits:
            found.update({m ^ bit: swap(piece, bit) for m, piece in found.items()})
        return found

    high, middle = team // 2, team // 4
    rest = [1 << b for b in range(team.bit_length() - 3)][::-1]
    class_map = mm(class_weight, down_weight, (((0,), (1,)), ((), ())))
    coarse = lax.reduce_precision(class_map, exponent_bits=8, mantissa_bits=7)
    parts = [x.astype(jnp.bfloat16) for x in (coarse, class_map - coarse)]
    up_weight = jnp.concatenate([up_weight, *parts], axis=0)
    sent = [pack(*tokens, *chunk, devices) for chunk in chunks[1:]]
    sent, up_weight, fixed, late, heads_in, pool = lax.optimization_barrier(
        (sent, up_weight, fixed, late, heads_in, pool)
    )
    gates = spread_out(gate_weight, [high, middle, *rest[:-1]])
    ups = spread_out(up_weight, [middle, high, *rest[:-1]])
    direct = [0, high, middle]
    sent, near_gates, near_ups = lax.optimization_barrier(
        (sent, [gates[m] for m in direct], [ups[m] for m in direct])
    )
    gates.update(zip(direct, near_gates))
    ups.update(zip(direct, near_ups))
    received += [exchange(x) for x in sent]

    def spread_out_again(found):
        found = {**found, **{m ^ 1: swap(piece, 1) for m, piece in found.items()}}
        return [found[m] for m in range(team)]

    attention = None
    pooled = []
    for qkv, (first, count) in zip(received, chunks):
        head = HEAD if first + count == slabs else 0
        attention, part = attend(
            qkv, pool, first, count, 2 * slabs, devices, rows, head, attention
        )
        if pooled:
            part, pooled[-1] = lax.optimization_barrier((part, pooled[-1]))
        else:
            part, gates, ups = lax.optimization_barrier((part, gates, ups))
            gates, ups = spread_out_again(gates), spread_out_again(ups)
        pooled.append(lax.all_to_all(part, "head", 0, 0, tiled=True))

    units = gate_weight.shape[1]

    inside = pl.BlockSpec(memory_space=pltpu.VMEM)
    outside = pl.BlockSpec(memory_space=pl.ANY)
    side = jax.ShapeDtypeStruct((team, total, units), jnp.bfloat16)
    members = [x for member in zip(gates, ups) for x in member]
    operands = [*pooled, *fixed, *late, *members]

    def buffers(xs):
        return [pltpu.VMEM(x.shape, x.dtype) for x in xs]

    partial, gate_side, up_side, own_x = pl.pallas_call(
        functools.partial(forward_kernel, [count * LANES for _, count in chunks], team, rows),
        out_shape=(
            jax.ShapeDtypeStruct((devices, showers, classes), jnp.float32),
            side,
            side,
            jax.ShapeDtypeStruct((block, width), jnp.float32),
        ),
        in_specs=[pl.BlockSpec(memory_space=pltpu.SMEM)] + [outside] * len(operands),
        out_specs=(inside, outside, outside, inside),
        scratch_shapes=buffers(operands)
        + [
            pltpu.VMEM((total, width), jnp.float32),
            pltpu.VMEM((total, width), jnp.bfloat16),
            pltpu.VMEM((LANES, LANES), jnp.float32),
            pltpu.VMEM(side.shape, side.dtype),
            pltpu.VMEM(side.shape, side.dtype),
            pltpu.SemaphoreType.DMA((len(operands),)),
            pltpu.SemaphoreType.DMA((2 * team,)),
        ],
        compiler_params=pltpu.CompilerParams(vmem_limit_bytes=58 * MIB),
        name="classifier_forward",
    )(jnp.stack([placed, me % team]).astype(jnp.int32), *operands)

    parts = lax.all_to_all(partial, "head", 0, 0, tiled=True)
    grads, miss = pl.pallas_call(
        functools.partial(backward_kernel, team),
        out_shape=(
            jax.ShapeDtypeStruct((outer, block, width), jnp.bfloat16),
            jax.ShapeDtypeStruct((showers, classes), jnp.float32),
        ),
        in_specs=[inside] * (1 + len(heads_in)) + [outside] * (len(members) + 2),
        scratch_shapes=buffers(members)
        + [
            pltpu.VMEM(side.shape, side.dtype),
            pltpu.VMEM(side.shape, side.dtype),
            pltpu.VMEM((total, width), jnp.float32),
            pltpu.SemaphoreType.DMA((4 * team,)),
        ],
        compiler_params=pltpu.CompilerParams(vmem_limit_bytes=58 * MIB),
        name="classifier_backward",
    )(parts, *heads_in, *members, gate_side, up_side)

    lines = [[o * team + m for o in range(outer)] for m in range(team)]
    grads = lax.all_to_all(grads, "head", 0, 0, axis_index_groups=lines, tiled=True)
    feature_grad = mm(miss, class_weight.astype(jnp.float32), NT, HIGH)
    here = here.reshape(showers, each, LANES)[:, :, :1] / shower_counts[:, None, None]
    own_row_grads = (here * feature_grad[:, None, :]).reshape(block, width)
    guidance = pl.pallas_call(
        functools.partial(final_kernel, float(windows)),
        out_shape=jax.ShapeDtypeStruct((showers, each, width), jnp.float32),
        compiler_params=pltpu.CompilerParams(vmem_limit_bytes=58 * MIB),
        name="norm_backward",
    )(grads, own_x, gain, scales, own_row_grads)
    return (attention.transpose(0, 2, 1), guidance)


def solution(mesh):
    in_specs = (
        P("parts", "head", None),
        P("parts", "head", None),
        P("parts", "head", None),
        P("parts", "head"),
        P("parts"),
        P("parts"),
        P("parts"),
        P(),
        P(),
        P(None, "head"),
        P(None, "head"),
        P("head", None),
        P(),
        P(),
    )
    out_specs = (P(("parts", "head"), None, None), P("parts", "head", None))
    return jax.shard_map(body, mesh=mesh, in_specs=in_specs, out_specs=out_specs, check_vma=False)
```

```python
import functools
import math

import jax
import jax.numpy as jnp
import numpy as np
from jax import lax
from jax.experimental import pallas as pl
from jax.experimental.pallas import tpu as pltpu
from jax.sharding import PartitionSpec as P

HEADS = 32
POOL = 16
LANES = 128
MASKED = -1e30
HEAD = 16
TEAM = 8
ABSENT = 64.0
epsilon = 1e-06
HIGH = lax.Precision.HIGHEST
NT = (((1,), (1,)), ((), ()))
TN = (((0,), (0,)), ((), ()))
NN = (((1,), (0,)), ((), ()))
MIB = 1 << 20


def mm(a, b, dims=NN, precision=None):
    return lax.dot_general(a, b, dims, precision=precision, preferred_element_type=jnp.float32)


def sinusoid(steps, embed_width):
    half_width = embed_width // 2
    frequency = jnp.exp(-math.log(10000.0) * jnp.arange(half_width, dtype=jnp.float32) / half_width)
    angles = steps.astype(jnp.float32)[:, None] * frequency[None, :]
    return jnp.concatenate([jnp.cos(angles), jnp.sin(angles)], axis=1)


def pack_kernel(first, count, slot_ref, count_ref, q_ref, k_ref, v_ref, out_ref, packed, sems, out_sems):
    showers, group, local, _ = packed.shape
    features = q_ref.shape[2] // group
    size = count * LANES
    arriving = []
    for m in range(group):
        at = m * features + first * LANES
        for t, ref in enumerate((q_ref, k_ref, v_ref)):
            place = packed.at[:, m, :, t * size : (t + 1) * size]
            copy = pltpu.make_async_copy(ref.at[:, :, at : at + size], place, sems.at[3 * m + t])
            copy.start()
            arriving.append(copy)
    square = (local, local)
    diagonal = lax.broadcasted_iota(jnp.int32, square, 0) == lax.broadcasted_iota(
        jnp.int32, square, 1
    )
    columns = []
    for s in range(showers):
        valid = (slot_ref[s : s + 1, :] < count_ref[s]).astype(jnp.float32)
        columns.append(jnp.sum(jnp.where(diagonal, valid, 0.0), axis=1, keepdims=True) > 0.5)
    leaving = []
    for m in range(group):
        for copy in arriving[3 * m : 3 * m + 3]:
            copy.wait()
        for s in range(showers):
            part = packed[s, m, :, size : 2 * size]
            packed[s, m, :, size : 2 * size] = jnp.where(
                columns[s], part, jnp.asarray(ABSENT, part.dtype)
            )
        copy = pltpu.make_async_copy(packed.at[:, m], out_ref.at[:, m], out_sems.at[m])
        copy.start()
        leaving.append(copy)
    for copy in leaving:
        copy.wait()


def pack(slot_positions, counts, queries, keys, values, first, count, devices):
    showers, local, width = queries.shape
    group = devices // showers
    shape = (showers, group, local, 3 * count * LANES)
    outside = pl.BlockSpec(memory_space=pl.ANY)
    packed = pl.pallas_call(
        functools.partial(pack_kernel, first, count),
        out_shape=jax.ShapeDtypeStruct(shape, jnp.bfloat16),
        in_specs=[
            pl.BlockSpec(memory_space=pltpu.VMEM),
            pl.BlockSpec(memory_space=pltpu.SMEM),
            outside,
            outside,
            outside,
        ],
        out_specs=outside,
        scratch_shapes=[
            pltpu.VMEM(shape, jnp.bfloat16),
            pltpu.SemaphoreType.DMA((3 * group,)),
            pltpu.SemaphoreType.DMA((group,)),
        ],
        compiler_params=pltpu.CompilerParams(vmem_limit_bytes=58 * MIB),
        name="pack",
    )(slot_positions, counts, queries, keys, values)
    return packed.reshape((devices,) + shape[2:])


def attend_kernel(block, head, q_ref, k_ref, v_ref, pool_ref, *rest):
    att_ref, pooled_ref = rest[-2:]
    length = q_ref.shape[0]
    half = LANES // 2
    lane = lax.broadcasted_iota(jnp.int32, (1, LANES), 1)
    low = lane < half
    keys = k_ref[...]
    rows = v_ref[...]
    one = jnp.ones_like(rows)
    wide_keys = keys.astype(jnp.float32)
    present = jnp.where(wide_keys < 0.5 * ABSENT, 1.0, 0.0).astype(jnp.bfloat16)
    pick = jnp.broadcast_to(jnp.where(lane == 0, 1.0, 0.0).astype(jnp.bfloat16), (8, LANES))
    valid = mm(pick, present, NT)[:1]
    marked = jnp.where(wide_keys < 0.5 * ABSENT, 0.0, MASKED)
    marked_keys = (
        jnp.where(low, wide_keys, jnp.where(lane == half, marked, 0.0)).astype(jnp.bfloat16),
        jnp.where(low, jnp.where(lane == 0, marked, 0.0), wide_keys).astype(jnp.bfloat16),
    )
    marks = [jnp.where(lane == at, 1.0, 0.0).astype(jnp.bfloat16) for at in (half, 0)]
    values = (jnp.where(low, rows, one), jnp.where(low, one, rows))

    for i in range(length // block):
        at = slice(i * block, (i + 1) * block)
        query = q_ref[at, :] * jnp.asarray(0.125, jnp.bfloat16)
        outs = []
        for h in range(2):
            mark = jnp.broadcast_to(marks[h], query.shape)
            own = jnp.where(low, query, mark) if h == 0 else jnp.where(low, mark, query)
            scores = mm(own, marked_keys[h], NT)
            peak = jnp.max(scores, axis=1, keepdims=True)
            weights = jnp.exp(scores - peak).astype(jnp.bfloat16)
            outs.append(mm(weights, values[h]))
        top = jnp.where(low, outs[0], outs[1])
        total = jnp.where(low, pltpu.roll(outs[0], half, 1), pltpu.roll(outs[1], half, 1))
        mixed = ((top / total).T * valid[:, at]).astype(jnp.bfloat16)
        att_ref[0, :, at] = mixed[:half]
        att_ref[1, :, at] = mixed[half:]
    both = jnp.concatenate([att_ref[0], att_ref[1]], axis=0)
    cnt = mm(pool_ref[...], jnp.broadcast_to(valid, (LANES, length)).astype(jnp.bfloat16), NT)
    pooled = (mm(pool_ref[...], both, NT) / jnp.maximum(cnt, 1.0)).astype(jnp.bfloat16)
    rows = pooled_ref.shape[1] - head
    team = pooled.shape[0] // rows
    if head:
        ones = jnp.broadcast_to(valid, (head, length)).astype(jnp.bfloat16)
        counted = mm(ones, pool_ref[...], NT).astype(jnp.bfloat16)
    for d in range(pooled_ref.shape[0]):
        m = d % team
        pooled_ref[d, head:] = pooled[m * rows : (m + 1) * rows]
        if head:
            pooled_ref[d, :head] = counted


def attend(qkv, pool, first, count, pairs, devices, rows, head, before):
    length = qkv.shape[0]
    windows = pool.shape[0]
    head_dim = LANES // 2

    def part(which):
        return pl.BlockSpec((length, LANES), lambda j: (0, which * count + j))

    def whole(shape):
        return pl.BlockSpec(shape, lambda j: (0, 0))

    in_specs = [
        part(0),
        part(1),
        part(2),
        whole((windows, length)),
    ]
    operands = [qkv, qkv, qkv, pool]
    aliases = {}
    if before is not None:
        in_specs.append(pl.BlockSpec(memory_space=pl.ANY))
        operands.append(before)
        aliases = {4: 0}
    return pl.pallas_call(
        functools.partial(attend_kernel, min(512, length), head),
        grid=(count,),
        out_shape=(
            jax.ShapeDtypeStruct((pairs, head_dim, length), jnp.bfloat16),
            jax.ShapeDtypeStruct((devices, head + rows, count * LANES), jnp.bfloat16),
        ),
        in_specs=in_specs,
        out_specs=(
            pl.BlockSpec((2, head_dim, length), lambda j: (first + j, 0, 0)),
            pl.BlockSpec((devices, head + rows, LANES), lambda j: (0, 0, j)),
        ),
        input_output_aliases=aliases,
        compiler_params=pltpu.CompilerParams(vmem_limit_bytes=40 * MIB),
        cost_estimate=pl.CostEstimate(
            flops=count * 2 * 4 * length * length * head_dim,
            bytes_accessed=count * length * LANES * 8,
            transcendentals=count * 2 * length * length,
        ),
        name="attend",
    )(*operands)


def split(x):
    coarse = x.astype(jnp.bfloat16)
    return coarse, (x - coarse.astype(jnp.float32)).astype(jnp.bfloat16)


def forward_kernel(lanes, team, rows, place_ref, *refs):
    n = len(lanes)
    inputs = n + 6 + 2 * team
    sources, (copies_ref, ga_out, aa_out, own_x_ref) = refs[:inputs], refs[inputs : inputs + 4]
    buffers = refs[inputs + 4 : 2 * inputs + 4]
    gathered, normed, counted, ga_ref, aa_ref, sems, out_sems = refs[2 * inputs + 4 :]
    arriving = [
        pltpu.make_async_copy(source, buffer, sems.at[i])
        for i, (source, buffer) in enumerate(zip(sources, buffers))
    ]
    first = n + 6
    for copy in arriving[: first + 2]:
        copy.start()

    def get(i):
        arriving[i].wait()
        return buffers[i]

    def start_member(i):
        if i < team:
            for copy in arriving[first + 2 * i : first + 2 * i + 2]:
                copy.start()

    showers, classes = copies_ref.shape[1:]
    group = buffers[0].shape[0] // showers
    width = gathered.shape[1]
    block = own_x_ref.shape[0]
    total = rows * showers
    x_refs = [get(i) for i in range(n)]
    start_member(1)
    for s in range(showers):
        for m in range(group):
            at = m * (width // group)
            for ref, size in zip(x_refs, lanes):
                part = ref[s * group + m, ref.shape[1] - rows :]
                gathered[s * rows : (s + 1) * rows, at : at + size] = part.astype(jnp.float32)
                at += size
    packed = gathered[...].astype(jnp.bfloat16)
    perm_ref, gain_ref, scale_ref, shift_ref = [get(n + i) for i in range(4)]
    gathered[...] = mm(perm_ref[...], packed)
    for b in range(total // block):
        at = slice(b * block, (b + 1) * block)
        x = gathered[at]
        inverse = lax.rsqrt(jnp.mean(x * x, axis=1, keepdims=True) + epsilon)
        normed[at] = (x * inverse * gain_ref[...] * scale_ref[...] + shift_ref[...]).astype(
            jnp.bfloat16
        )
    own_x_ref[...] = gathered[pl.ds(pl.multiple_of(place_ref[0] * block, block), block), :]
    counts_ref, class_ref = [get(n + 4 + i) for i in range(2)]
    counted[...] = jnp.zeros(counted.shape, jnp.float32)
    for s in range(showers):
        counted[s : s + 1] = x_refs[-1][s * group, :HEAD].astype(jnp.float32)[:1]
    shape = (total, LANES)
    row = lax.broadcasted_iota(jnp.int32, shape, 0)
    lane = lax.broadcasted_iota(jnp.int32, shape, 1)
    each = block // showers
    from_lane = place_ref[1] * rows + row // block * each + row % each
    pick = jnp.where(lane == from_lane, 1.0, 0.0).astype(jnp.bfloat16)
    cnt_of = mm(pick, counted[...].astype(jnp.bfloat16), NT)
    cnt_of = jnp.where(lane == row % block // each, cnt_of, 0.0)
    cnt = jnp.sum(cnt_of, axis=1, keepdims=True)
    own_cnt_of = jnp.where(row // block == place_ref[0], cnt_of, 0.0).astype(jnp.bfloat16)
    cnt_of = cnt_of.astype(jnp.bfloat16)
    sums = mm(own_cnt_of, gathered[...].astype(jnp.bfloat16), TN)[:showers]
    logits = mm(sums, class_ref[...].astype(jnp.float32), precision=HIGH)
    coef = cnt / counts_ref[...][:, :1]
    leaving = []

    def finish(i, gate, up, logits):
        up_ref = buffers[first + 2 * i + 1]
        sigma = jax.nn.sigmoid(gate)
        activated = gate * sigma
        hidden = (activated * up).astype(jnp.bfloat16)
        ga_ref[i] = (coef * (up * sigma * (1.0 + gate * (1.0 - sigma)))).astype(jnp.bfloat16)
        aa_ref[i] = (coef * activated).astype(jnp.bfloat16)
        for j, (kept, out) in enumerate(((ga_ref, ga_out), (aa_ref, aa_out))):
            copy = pltpu.make_async_copy(kept.at[i], out.at[i], out_sems.at[2 * i + j])
            copy.start()
            leaving.append(copy)
        coarse, fine = split(mm(cnt_of, hidden, TN)[:showers])
        both = mm(coarse, up_ref[width:], NT)
        logits = logits + both[:, :classes] + both[:, classes:]
        return logits + mm(fine, up_ref[width : width + classes], NT)

    before = None
    for i in range(team):
        gate_ref, up_ref = [get(first + 2 * i + j) for j in range(2)]
        start_member(i + 2)
        gate = mm(normed[...], gate_ref[...])
        up = mm(normed[...], up_ref[:width])
        if before is not None:
            logits = finish(i - 1, *before, logits)
        before = (gate, up)
    logits = finish(team - 1, *before, logits)
    for d in range(copies_ref.shape[0]):
        copies_ref[d] = logits
    for copy in leaving:
        copy.wait()


def backward_kernel(team, parts_ref, counts_ref, bias_ref, target_ref, spread_ref, *refs):
    sources = refs[: 2 * team]
    ga_in, aa_in, dn_ref, miss_ref = refs[2 * team : 2 * team + 4]
    buffers = refs[2 * team + 4 : 4 * team + 4]
    ga_ref, aa_ref, total, sems = refs[4 * team + 4 :]
    arriving = []
    for i in range(team):
        pairs = [(ga_in.at[i], ga_ref.at[i]), (aa_in.at[i], aa_ref.at[i])]
        pairs += [(sources[2 * i + j], buffers[2 * i + j]) for j in range(2)]
        arriving.append(
            [
                pltpu.make_async_copy(source, buffer, sems.at[4 * i + j])
                for j, (source, buffer) in enumerate(pairs)
            ]
        )

    def start_member(i):
        if i < team:
            for copy in arriving[i]:
                copy.start()

    start_member(0)
    start_member(1)
    blocks, block, _ = dn_ref.shape
    logits = jnp.sum(parts_ref[...], axis=0) / counts_ref[...] + bias_ref[...]
    exponent = jnp.exp(logits - jnp.max(logits, axis=1, keepdims=True))
    miss = target_ref[...] - exponent / jnp.sum(exponent, axis=1, keepdims=True)
    miss_ref[...] = miss
    coarse, fine = split(mm(spread_ref[...], miss, precision=HIGH))
    coarse = jnp.concatenate([coarse, coarse], axis=1)
    classes = miss.shape[1]
    width = dn_ref.shape[2]
    for i in range(team):
        gate_ref, up_ref = buffers[2 * i : 2 * i + 2]
        for copy in arriving[i]:
            copy.wait()
        start_member(i + 2)
        wide = mm(coarse, up_ref[width:]) + mm(fine, up_ref[width : width + classes])
        wide = jnp.concatenate([wide] * blocks, axis=0)
        gate_grad = (wide * ga_ref[i].astype(jnp.float32)).astype(jnp.bfloat16)
        up_grad = (wide * aa_ref[i].astype(jnp.float32)).astype(jnp.bfloat16)
        term = mm(gate_grad, gate_ref[...], NT) + mm(up_grad, up_ref[:width], NT)
        if i == 0:
            total[...] = term
        elif i < team - 1:
            total[...] += term
        else:
            term = (total[...] + term).astype(jnp.bfloat16)
            for b in range(blocks):
                dn_ref[b] = term[b * block : (b + 1) * block]


def final_kernel(windows, dn_ref, x_ref, gain_ref, scale_ref, dy_ref, out_ref):
    total = dn_ref[0].astype(jnp.float32)
    for b in range(1, dn_ref.shape[0]):
        total = total + dn_ref[b].astype(jnp.float32)
    x = x_ref[...]
    inverse = lax.rsqrt(jnp.mean(x * x, axis=1, keepdims=True) + epsilon)
    unit = x * inverse
    grad = total * gain_ref[...] * scale_ref[...]
    back = inverse * (grad - unit * jnp.mean(grad * unit, axis=1, keepdims=True))
    value = windows * (dy_ref[...] + back)
    each = out_ref.shape[1]
    for s in range(out_ref.shape[0]):
        out_ref[s] = value[s * each : (s + 1) * each]


def body(
    queries,
    keys,
    values,
    slot_positions,
    counts,
    timesteps,
    labels,
    time_weight,
    norm_gain,
    gate_weight,
    up_weight,
    down_weight,
    class_weight,
    class_bias,
):
    devices = lax.axis_size("head")
    me = lax.axis_index("head")
    showers, local, width = queries.shape
    length = local * devices
    group = devices // showers
    team = TEAM
    outer = devices // team
    features = width // group
    slabs = features // LANES
    each = local // POOL
    windows = length // POOL
    classes = class_weight.shape[1]
    placed = me // team
    rows = outer * each
    block = showers * each
    total = showers * rows

    def swap(x, bit):
        return lax.ppermute(x, "head", [(d, d ^ bit) for d in range(devices)])

    chunks = [(0, slabs - 1), (slabs - 1, 1)] if slabs > 1 else [(0, 1)]

    valid = (slot_positions < counts[:, None]).astype(jnp.float32)
    here = jnp.sum(valid.reshape(block, POOL), axis=1, keepdims=True)
    here = jnp.broadcast_to(here, (block, LANES))

    tokens = (slot_positions, counts, queries, keys, values)
    sent = pack(*tokens, *chunks[0], devices)

    def exchange(x):
        got = lax.all_to_all(x, "head", 0, 0, tiled=True)
        return got.reshape(length, x.shape[2])

    received = [exchange(sent)]

    order = np.arange(windows).reshape(outer, team, each).transpose(1, 0, 2).reshape(windows)
    pool = jnp.asarray(order, jnp.int32)[:, None] == jnp.arange(length, dtype=jnp.int32)[None] // POOL
    pool = pool.astype(jnp.bfloat16)

    shower_counts = counts.astype(jnp.float32)
    row_counts = jnp.tile(jnp.repeat(shower_counts, each), outer)
    row_counts = jnp.broadcast_to(row_counts[:, None], (total, LANES))
    source = np.arange(total).reshape(showers, outer, each).transpose(1, 0, 2).reshape(total)
    perm = jnp.asarray(source, jnp.int32)[:, None] == jnp.arange(total, dtype=jnp.int32)[None]
    perm = perm.astype(jnp.bfloat16)
    embedding = sinusoid(timesteps, time_weight.shape[0]).astype(jnp.bfloat16)
    modulation = jnp.dot(embedding, time_weight, preferred_element_type=jnp.float32)
    shifts = jnp.repeat(modulation[:, :width], each, axis=0)
    scales = jnp.repeat(1.0 + modulation[:, width:], each, axis=0)
    gain = norm_gain.reshape(1, width)

    target = (labels[:, None] == jnp.arange(classes, dtype=jnp.int32)[None]).astype(jnp.float32)
    spread = jnp.asarray(
        np.repeat(np.eye(showers), each, axis=0).astype(np.float32)
    )
    spread_counts = jnp.broadcast_to(shower_counts[:, None], (showers, classes))
    heads_in = (spread_counts, class_bias.reshape(1, classes), target, spread)
    fixed = (perm, gain, scales, shifts)
    late = (row_counts, class_weight)
    def spread_out(x, bits):
        found = {0: x}
        for bit in bits:
            found.update({m ^ bit: swap(piece, bit) for m, piece in found.items()})
        return found

    high, middle = team // 2, team // 4
    rest = [1 << b for b in range(team.bit_length() - 3)][::-1]
    class_map = mm(class_weight, down_weight, (((0,), (1,)), ((), ())))
    coarse = lax.reduce_precision(class_map, exponent_bits=8, mantissa_bits=7)
    parts = [x.astype(jnp.bfloat16) for x in (coarse, class_map - coarse)]
    up_weight = jnp.concatenate([up_weight, *parts], axis=0)
    sent = [pack(*tokens, *chunk, devices) for chunk in chunks[1:]]
    sent, up_weight, fixed, late, heads_in, pool = lax.optimization_barrier(
        (sent, up_weight, fixed, late, heads_in, pool)
    )
    gates = spread_out(gate_weight, [high, middle, *rest[:-1]])
    ups = spread_out(up_weight, [middle, high, *rest[:-1]])
    direct = [0, high, middle]
    sent, near_gates, near_ups = lax.optimization_barrier(
        (sent, [gates[m] for m in direct], [ups[m] for m in direct])
    )
    gates.update(zip(direct, near_gates))
    ups.update(zip(direct, near_ups))
    received += [exchange(x) for x in sent]

    def cross(found, members):
        found.update({m ^ 1: swap(found[m], 1) for m in members})

    far = [m for m in gates if m not in direct]
    attention = None
    pooled = []
    for qkv, (first, count) in zip(received, chunks):
        head = HEAD if first + count == slabs else 0
        attention, part = attend(
            qkv, pool, first, count, 2 * slabs, devices, rows, head, attention
        )
        if pooled:
            part, pooled[-1] = lax.optimization_barrier((part, pooled[-1]))
        if not pooled:
            _, near_gates, near_ups = lax.optimization_barrier(
                (part, [gates[m] for m in direct], [ups[m] for m in direct])
            )
            gates.update(zip(direct, near_gates))
            ups.update(zip(direct, near_ups))
            cross(gates, direct)
            cross(ups, direct)
        if first + count == slabs:
            _, far_gates, far_ups = lax.optimization_barrier(
                (part, [gates[m] for m in far], [ups[m] for m in far])
            )
            gates.update(zip(far, far_gates))
            ups.update(zip(far, far_ups))
            cross(gates, far)
            cross(ups, far)
        pooled.append(lax.all_to_all(part, "head", 0, 0, tiled=True))

    units = gate_weight.shape[1]

    inside = pl.BlockSpec(memory_space=pltpu.VMEM)
    outside = pl.BlockSpec(memory_space=pl.ANY)
    side = jax.ShapeDtypeStruct((team, total, units), jnp.bfloat16)
    members = [x for m in range(team) for x in (gates[m], ups[m])]
    operands = [*pooled, *fixed, *late, *members]

    def buffers(xs):
        return [pltpu.VMEM(x.shape, x.dtype) for x in xs]

    partial, gate_side, up_side, own_x = pl.pallas_call(
        functools.partial(forward_kernel, [count * LANES for _, count in chunks], team, rows),
        out_shape=(
            jax.ShapeDtypeStruct((devices, showers, classes), jnp.float32),
            side,
            side,
            jax.ShapeDtypeStruct((block, width), jnp.float32),
        ),
        in_specs=[pl.BlockSpec(memory_space=pltpu.SMEM)] + [outside] * len(operands),
        out_specs=(inside, outside, outside, inside),
        scratch_shapes=buffers(operands)
        + [
            pltpu.VMEM((total, width), jnp.float32),
            pltpu.VMEM((total, width), jnp.bfloat16),
            pltpu.VMEM((LANES, LANES), jnp.float32),
            pltpu.VMEM(side.shape, side.dtype),
            pltpu.VMEM(side.shape, side.dtype),
            pltpu.SemaphoreType.DMA((len(operands),)),
            pltpu.SemaphoreType.DMA((2 * team,)),
        ],
        compiler_params=pltpu.CompilerParams(vmem_limit_bytes=58 * MIB),
        name="classifier_forward",
    )(jnp.stack([placed, me % team]).astype(jnp.int32), *operands)

    parts = lax.all_to_all(partial, "head", 0, 0, tiled=True)
    grads, miss = pl.pallas_call(
        functools.partial(backward_kernel, team),
        out_shape=(
            jax.ShapeDtypeStruct((outer, block, width), jnp.bfloat16),
            jax.ShapeDtypeStruct((showers, classes), jnp.float32),
        ),
        in_specs=[inside] * (1 + len(heads_in)) + [outside] * (len(members) + 2),
        scratch_shapes=buffers(members)
        + [
            pltpu.VMEM(side.shape, side.dtype),
            pltpu.VMEM(side.shape, side.dtype),
            pltpu.VMEM((total, width), jnp.float32),
            pltpu.SemaphoreType.DMA((4 * team,)),
        ],
        compiler_params=pltpu.CompilerParams(vmem_limit_bytes=58 * MIB),
        name="classifier_backward",
    )(parts, *heads_in, *members, gate_side, up_side)

    lines = [[o * team + m for o in range(outer)] for m in range(team)]
    grads = lax.all_to_all(grads, "head", 0, 0, axis_index_groups=lines, tiled=True)
    feature_grad = mm(miss, class_weight.astype(jnp.float32), NT, HIGH)
    here = here.reshape(showers, each, LANES)[:, :, :1] / shower_counts[:, None, None]
    own_row_grads = (here * feature_grad[:, None, :]).reshape(block, width)
    guidance = pl.pallas_call(
        functools.partial(final_kernel, float(windows)),
        out_shape=jax.ShapeDtypeStruct((showers, each, width), jnp.float32),
        compiler_params=pltpu.CompilerParams(vmem_limit_bytes=58 * MIB),
        name="norm_backward",
    )(grads, own_x, gain, scales, own_row_grads)
    return (attention.transpose(0, 2, 1), guidance)


def solution(mesh):
    in_specs = (
        P("parts", "head", None),
        P("parts", "head", None),
        P("parts", "head", None),
        P("parts", "head"),
        P("parts"),
        P("parts"),
        P("parts"),
        P(),
        P(),
        P(None, "head"),
        P(None, "head"),
        P("head", None),
        P(),
        P(),
    )
    out_specs = (P(("parts", "head"), None, None), P("parts", "head", None))
    return jax.shard_map(body, mesh=mesh, in_specs=in_specs, out_specs=out_specs, check_vma=False)
```
